512 devices in a mesh: axial: 16 (over y, x), azim: 32 (over z, core).
Axes of the slice: x: 4, y: 4, z: 16, core: 2. Of those that a mesh axis runs over, the one named last changes fastest.
Arguments:
- gas_state: float32 [4, 8192, 4096], P(None, 'axial', 'azim'), may hold values from -6 to 6
- mean_flow: float32 [8192, 4096], P('axial', 'azim'), may hold values from 0.05 to 0.5
- part_target: float32 [16384, 4, 128], P(('axial', 'azim')), may hold values from -6 to 6
- part_offset: float32 [16384, 128], P(('axial', 'azim')), may hold values from 0 to 1
- part_width: float32 [16384, 128], P(('axial', 'azim')), may hold values from 0.6 to 2
- part_rate: float32 [16384, 128], P(('axial', 'azim')), may hold values from 0.1 to 1
- cell_index: int32 [16384, 128], P(('axial', 'azim')), may hold values from 0 to 127
- dest_owner: int32 [16384, 1], P(('axial', 'azim')), may hold values from 0 to 31; in each aligned block of 32 rows (0 to 31, 32 to 63, ...) at most 2 rows name the same one
- gas_row: int32 [16384], P(('axial', 'azim')), may hold values from 0 to 511
- live_count: int32 [512], P(('axial', 'azim')), may hold values from 512 to 4096
Outputs:
- new_state: float32 [4, 8192, 4096], P(None, 'axial', 'azim')
The draws below stay inside these ranges and needn't reach their ends.
Inputs may be any that keep to these rules, and one draw needn't show every extreme that they name: `dest_owner`: at most 2 of the 32 tiles of one surface owner name the same sector.
All inputs are finite; a program needn't handle non-finite values.
Results may differ from the reference program's by a relative error of at most 0.0001.
Values sent between devices are 32-bit elements; how exact they have to be, the bound alone decides.
No kernel may reach another device: no remote copies, remote signals or barrier semaphores. Data moves between devices by JAX's collectives and lax.ppermute only.
A program may use at most 64 MiB of HBM per device.

```python
import math
import jax
import jax.numpy as jnp
import numpy as np
from jax import lax

VARS = 4
TILE = 128
CA = 512
CAP = 2
TILES_DEV = 32
NA = 8192
NB = 4096
OWNERS = 512
TILES = 16384
N_AXIAL = 16
N_AZIM = 32


def draw_live_count(key, part):
    key = jax.random.fold_in(key, 11)
    key_vals, key_top, key_low = jax.random.split(key, 3)
    most = TILES_DEV * TILE
    least = TILES_DEV * TILE // 8
    factor = jax.random.randint(key_vals, (OWNERS,), 3, 9)
    counts = least * factor * factor // 8
    top_index = jax.random.randint(key_top, (), 0, OWNERS)
    low_index = (top_index + 1 + jax.random.randint(key_low, (), 0, OWNERS - 1)) % OWNERS
    counts = counts.at[top_index].set(most)
    counts = counts.at[low_index].set(least)
    return counts.astype(jnp.int32)


def with_ends(array, key, smallest, top_value):
    extent = array.shape
    spot = [jax.random.randint(jax.random.fold_in(key, axis), (), 0, extent[axis]) for axis in range(len(extent))]
    array = array.at[tuple(spot)].set(smallest)
    longest = extent.index(max(extent))
    spot[longest] = (spot[longest] + 1) % extent[longest]
    return array.at[tuple(spot)].set(top_value)


def levels(stream_key, shape, cuts, low, top_value):
    loudness = 1.0
    for axis_at, blocks in cuts:
        heights = jax.random.uniform(jax.random.fold_in(jax.random.fold_in(stream_key, 6), axis_at), (blocks,), jnp.float32, low / len(cuts), top_value / len(cuts))
        loudness = loudness * jnp.repeat(jnp.exp(heights), shape[axis_at] // blocks).reshape((-1,) + (1,) * (len(shape) - 1 - axis_at))
    return loudness


def routed_block(rng, own, number, rows, number_of, top, bound, lean):
    ranking = jax.random.permutation(rng, number_of)
    packed, ordinary = shares(number_of, rows * top, bound, lean, True), shares(number_of, rows * top, bound, lean, False)
    places = jnp.arange(number_of)

    def named(tallies, offset_by):
        used = int((tallies > 0).sum())
        fixed = max(1, used // 4)
        passed = fixed + (places - fixed + offset_by * (used - fixed)) % max(1, number_of - fixed)
        return jnp.zeros((number_of,), jnp.int32).at[ranking[jnp.where(places < fixed, places, passed)]].set(jnp.asarray(tallies, jnp.int32))

    tallies = jnp.where(number % 4 == 0, named(packed, number // 4), named(ordinary, number - number // 4 - 1))
    mixed = jax.random.permutation(jax.random.fold_in(own, 3), number_of)
    donor, taker = mixed[0:number_of // 2 * 2:2], mixed[1:number_of // 2 * 2:2]
    slack = jnp.minimum(tallies[donor] - 1, bound - tallies[taker]) // 2
    slack = jnp.where((donor == ranking[0]) | (taker == ranking[0]) | (tallies[taker] == 0), 0, jnp.maximum(slack, 0))
    passed = jax.random.randint(jax.random.fold_in(own, 4), (number_of // 2,), 0, 1 << 20) % (slack + 1)
    tallies = tallies.at[donor].add(-passed).at[taker].add(passed)
    labels = jnp.searchsorted(jnp.cumsum(tallies), jnp.arange(rows * top), side="right").astype(jnp.int32)
    table = labels.reshape(top, rows).T
    table = table[jax.random.permutation(jax.random.fold_in(own, 1), rows)]
    offset_by = jax.random.randint(jax.random.fold_in(own, 2), (rows, 1), 0, top)
    return jnp.take_along_axis(table, (jnp.arange(top)[None, :] + offset_by) % top, axis=1)


def shares(number_of, total, reach, lean, full):
    loads = [(1 << 20) // math.isqrt(rank ** lean) + 1 for rank in range(1, number_of + 1)]
    largest = reach if full else min(reach, max(-(-total // number_of), total * loads[0] // sum(loads)))
    least = 1 if total - largest >= number_of - 1 else 0
    holding, surplus = [largest] + [least] * (number_of - 1), total - largest - least * (number_of - 1)
    while surplus > 0:
        candidates = [i for i in range(1, number_of) if holding[i] < largest] or [i for i in range(1, number_of) if holding[i] < reach]
        whole, remaining = sum([loads[i] for i in candidates]), surplus
        for i in candidates:
            addition = min(reach - holding[i], max(1, remaining * loads[i] // whole), surplus)
            holding[i] = holding[i] + addition
            surplus = surplus - addition
    return np.array(holding)


def bell_draw(key, extent, scale, reach, shards=(), dtype=jnp.bfloat16):
    array = jax.random.normal(key, extent, jnp.float32) * scale
    if len(shards) > 0:
        array = levels(key, extent, shards, -0.22, 0.18) * array
    return jnp.clip(array, min=-reach, max=reach).astype(dtype)


def setup_inputs(seed: int = 0) -> dict:
    splits = jax.random.split(jax.random.key(seed), 11)
    gas_state = bell_draw(splits[0], (VARS, NA, NB), 1.0, 6.0, ((1, 16), (2, 32)), jnp.float32)
    mean_flow = jnp.clip(jnp.exp(math.log(0.5) - 2.3025851 * jax.random.uniform(splits[1], (NA, NB), jnp.float32) ** levels(splits[1], (NA, NB), ((0, 16), (1, 32)), -0.2, 0.2)), 0.05, 0.5)
    part_target = bell_draw(splits[2], (TILES, VARS, TILE), 1.0, 6.0, ((0, 512),), jnp.float32)
    part_offset = jnp.clip(1.0 * jax.random.uniform(splits[3], (TILES, TILE), jnp.float32) ** levels(splits[3], (TILES, TILE), ((0, 512),), -0.2, 0.2), 0.0, 1.0)
    part_width = jnp.clip(jnp.exp(math.log(2.0) - 1.2039728 * jax.random.uniform(splits[4], (TILES, TILE), jnp.float32) ** levels(splits[4], (TILES, TILE), ((0, 512),), -0.2, 0.2)), 0.6, 2.0)
    part_rate = jnp.clip(jnp.exp(math.log(1.0) - 2.3025851 * jax.random.uniform(splits[5], (TILES, TILE), jnp.float32) ** levels(splits[5], (TILES, TILE), ((0, 512),), -0.2, 0.2)), 0.1, 1.0)
    cell_index = with_ends(jax.random.randint(splits[6], (TILES, TILE), 0, TILE), jax.random.fold_in(splits[6], 1), 0, TILE - 1).astype(jnp.int32)
    dest_owner_keys = jax.random.split(jax.random.fold_in(splits[7], 1), TILES // TILES_DEV)
    dest_owner_turns = jax.random.permutation(jax.random.fold_in(splits[7], 3), TILES // TILES_DEV)
    dest_owner = jax.vmap(lambda own, number: routed_block(jax.random.fold_in(splits[7], 2), own, number, TILES_DEV, N_AZIM, 1, CAP, 2))(dest_owner_keys, dest_owner_turns).reshape((TILES, 1))
    gas_row = with_ends(jax.random.randint(splits[8], (TILES,), 0, CA), jax.random.fold_in(splits[8], 1), 0, CA - 1).astype(jnp.int32)
    live_count = draw_live_count(jax.random.fold_in(splits[10], 71), 0)
    return {"gas_state": gas_state, "mean_flow": mean_flow, "part_target": part_target, "part_offset": part_offset, "part_width": part_width, "part_rate": part_rate, "cell_index": cell_index, "dest_owner": dest_owner, "gas_row": gas_row, "live_count": live_count}


time_step = 0.8


def build_tiles(cell_ids, offsets, widths):
    width_t = cell_ids.shape[-1]
    centre = cell_ids.astype(jnp.float32) + offsets
    cell_mid = jnp.arange(width_t).astype(jnp.float32) + 0.5
    cell_gap = cell_mid[None, None, :] - centre[:, :, None]
    weight = jnp.exp(-cell_gap * cell_gap / (2.0 * widths[:, :, None] * widths[:, :, None]))
    return weight / jnp.sum(weight, axis=2, keepdims=True)


def reference(gas_state, mean_flow, part_target, part_offset, part_width, part_rate, cell_index, dest_owner, gas_row, live_count):
    tiles_all = TILES_DEV * N_AXIAL * N_AZIM
    tile_ids = jnp.arange(tiles_all).astype(jnp.int32)
    owner_ids = tile_ids // TILES_DEV
    local_tile = tile_ids % TILES_DEV
    particle = local_tile[:, None] * TILE + jnp.arange(TILE).astype(jnp.int32)[None, :]
    is_live = particle < live_count[owner_ids][:, None]
    live_rate = jnp.where(is_live, part_rate, jnp.zeros_like(part_rate))
    global_row = (owner_ids // N_AZIM) * CA + gas_row
    sector_ids = dest_owner[:, 0]
    group_size = N_AZIM * TILES_DEV
    pieces = (global_row.reshape(N_AXIAL, group_size),
              sector_ids.reshape(N_AXIAL, group_size),
              cell_index.reshape(N_AXIAL, group_size, TILE),
              part_offset.reshape(N_AXIAL, group_size, TILE),
              part_width.reshape(N_AXIAL, group_size, TILE),
              live_rate.reshape(N_AXIAL, group_size, TILE),
              part_target.reshape(N_AXIAL, group_size, VARS, TILE))

    def coupling(section_state):
        grid_view = section_state.reshape(VARS, NA, N_AZIM, TILE)

        def one_group(summed, group_parts):
            row_ids, sectors, cell_ids, offsets, widths, rate_vals, targets = group_parts
            tile_set = build_tiles(cell_ids, offsets, widths)
            sampled = grid_view[:, row_ids, sectors, :]
            guessed = jnp.einsum('kbc,bjc->bkj', sampled, tile_set, precision=lax.Precision.HIGHEST)
            forcing = rate_vals[:, None, :] * (targets - guessed)
            source = jnp.einsum('bkj,bjc->kbc', forcing, tile_set, precision=lax.Precision.HIGHEST)
            return summed.at[:, row_ids, sectors, :].add(source), None

        summed, _ = lax.scan(one_group, jnp.zeros_like(grid_view), pieces)
        return summed.reshape(VARS, NA, NB)

    def tendency(section_state):
        padded = jnp.pad(section_state, ((0, 0), (1, 1), (0, 0)))
        padded = jnp.concatenate([padded[:, :, -1:], padded, padded[:, :, :1]], axis=2)
        axial_diff = 0.5 * (padded[:, 2:, 1:-1] - padded[:, :-2, 1:-1])
        azim_diff = 0.5 * (padded[:, 1:-1, 2:] - padded[:, 1:-1, :-2])
        divergence = axial_diff[1] + azim_diff[2]
        waves = jnp.stack([divergence, axial_diff[3], azim_diff[3], divergence])
        change = -mean_flow[None] * axial_diff - waves
        return change + coupling(section_state)

    section_one = gas_state + time_step * tendency(gas_state)
    section_two = 0.75 * gas_state + 0.25 * (section_one + time_step * tendency(section_one))
    return gas_state / 3.0 + (2.0 / 3.0) * (section_two + time_step * tendency(section_two))
```

```python
import math

import jax
import jax.numpy as jnp
from jax import lax
from jax.experimental import pallas as pl
from jax.experimental.pallas import tpu as pltpu
from jax.sharding import PartitionSpec as P

CAP = 2
CELLS = 128
VARS = 4
TOP = 8
CHUNK = 32
VMEM_BYTES = 20 * 1024 * 1024

time_step = 0.8
quarter = 0.25 * time_step
eighth = 0.125 * time_step

f32 = jnp.float32
bf16 = jnp.bfloat16


def vmem():
    return pl.BlockSpec(memory_space=pltpu.VMEM)


def smem():
    return pl.BlockSpec(memory_space=pltpu.SMEM)


def shape(dims, dtype=f32):
    return jax.ShapeDtypeStruct(dims, dtype)


def lanes_of(rows):
    return lax.broadcasted_iota(jnp.int32, (rows, CELLS), 1)


def slots_kernel(dest, gas_row, live, target, offset, width, rate, cell, send, centre_of, factor_of, live_of, used):
    tiles = offset.shape[0]
    sectors = send.shape[0] // CAP
    send[...] = jnp.zeros(send.shape, f32)
    centre_of[...] = cell[...].astype(f32) + offset[...]
    factor_of[...] = (-0.5 / math.log(2.0)) / (width[...] * width[...])
    particle = lax.broadcasted_iota(jnp.int32, (tiles, CELLS), 0) * CELLS + lanes_of(tiles)
    live_of[...] = jnp.where(particle < live[0], rate[...], 0.0)
    for s in range(sectors):
        used[s] = 0
    for t in range(tiles):
        sector = dest[t]
        earlier = used[sector]
        used[sector] = earlier + 1
        slot = sector * CAP + earlier
        send[slot, 0:1, :] = centre_of[t : t + 1, :]
        send[slot, 1:2, :] = factor_of[t : t + 1, :]
        send[slot, 2:3, :] = live_of[t : t + 1, :]
        send[slot, 3:4, :] = jnp.full((1, CELLS), gas_row[t].astype(f32))
        send[slot, 4:8, :] = target[t]


def turned(columns):
    lane = lanes_of(CELLS)
    total = jnp.zeros((CELLS, CELLS), f32)
    for i, column in enumerate(columns):
        total = jnp.where(lane == i, column, total)
    return total.T


def edge_columns(cells, first, lane):
    blocks = (cells.shape[1] - 2 * first) // CELLS
    return [
        cells[k, first + CELLS * b : first + CELLS * (b + 1), lane : lane + 1] for k in (2, 3) for b in range(blocks)
    ]


def edges_kernel(state, flow, down, up, right, left):
    rows = state.shape[1]
    for out, r in ((up, 0), (down, rows - 1)):
        for k in range(VARS):
            out[k : k + 1, :] = state[k, r : r + 1, :]
        out[4:5, :] = flow[r : r + 1, :]
        out[5:8, :] = jnp.ones((3, CELLS), f32)
    both = turned(edge_columns(state, 0, 0) + edge_columns(state, 0, CELLS - 1))
    left[...] = both[0:8, :]
    right[...] = both[8:16, :]


def chunk_rates(cells, flow, sides, r0, left_at, right_at):
    lane = lanes_of(CHUNK)
    here = slice(TOP + r0, TOP + r0 + CHUNK)
    dx = [
        0.5 * (cells[k, TOP + r0 + 1 : TOP + r0 + CHUNK + 1, :] - cells[k, TOP + r0 - 1 : TOP + r0 + CHUNK - 1, :])
        for k in range(VARS)
    ]
    dy = []
    block, within = r0 // CELLS, r0 % CELLS
    for k in (2, 3):
        cell = cells[k, here, :]
        if sides is None:
            before, after = 0.0, 0.0
        else:
            place = 4 * (k - 2) + block
            before = sides[within : within + CHUNK, left_at + place : left_at + place + 1]
            after = sides[within : within + CHUNK, right_at + place : right_at + place + 1]
        west = jnp.where(lane == 0, before, pltpu.roll(cell, 1, 1))
        east = jnp.where(lane == CELLS - 1, after, pltpu.roll(cell, CELLS - 1, 1))
        dy.append(0.5 * (east - west))
    speed = flow[r0 : r0 + CHUNK, :]
    spread = dx[1] + dy[0]
    return [
        -speed * dx[0] - spread,
        -speed * dx[1] - dx[3],
        -speed * dx[2] - dy[1],
        -speed * dx[3] - spread,
    ]


def fill_rows(cells, top, bottom):
    rows = cells.shape[1] - 2 * TOP
    for k in range(VARS):
        cells[k, TOP - 1 : TOP, :] = top[k]
        cells[k, TOP + rows : TOP + rows + 1, :] = bottom[k]


def waves_kernel(state, flow, above, below, from_left, from_right, out, padded, sides):
    rows = state.shape[1]
    padded[:, TOP : TOP + rows, :] = state[...]
    fill_rows(padded, [above[k : k + 1, :] for k in range(VARS)], [below[k : k + 1, :] for k in range(VARS)])
    sides[...] = jnp.concatenate([from_left[...], from_right[...], jnp.zeros((CELLS - 16, CELLS), f32)], 0).T
    for r0 in range(0, rows, CHUNK):
        rates = chunk_rates(padded, flow, sides, r0, 0, 8)
        for k in range(VARS):
            out[k, TOP + r0 : TOP + r0 + CHUNK, :] = state[k, r0 : r0 + CHUNK, :] + time_step * rates[k]
    fill_rows(out, [jnp.zeros((1, CELLS), f32)] * VARS, [jnp.zeros((1, CELLS), f32)] * VARS)


def sample(cells, first, row_of, samples):
    for t in range(samples.shape[0] // 8):
        r = row_of[0, t] + first
        for k in range(VARS):
            line = cells[k, pl.ds(r, 1), :]
            samples[8 * t + k : 8 * t + k + 1, :] = line
            samples[8 * t + 4 + k : 8 * t + 5 + k, :] = line


def high_and_low(values):
    high = values.astype(bf16).astype(f32)
    low_row = lax.broadcasted_iota(jnp.int32, values.shape, 0) % 8 >= 4
    return jnp.where(low_row, values - high, high)


def add_sources(samples, weights, goals, rates, row_of, out, first, scale):
    nothing = jnp.zeros((8, CELLS), f32)
    for p in range(weights.shape[0]):
        seen = high_and_low(samples[16 * p : 16 * p + 16, :]).astype(bf16)
        guess = jnp.dot(jnp.concatenate([seen, seen], 1), weights[p], preferred_element_type=f32)
        forces = []
        for i in range(2):
            part = guess[8 * i : 8 * i + 8, CELLS * i : CELLS * (i + 1)]
            part = part + pltpu.roll(part, 4, 0)
            forces.append(high_and_low(goals[2 * p + i] - rates[2 * p + i] * part))
        forces = jnp.concatenate(
            [jnp.concatenate([forces[0], nothing], 1), jnp.concatenate([nothing, forces[1]], 1)], 0
        ).astype(bf16)
        both = lax.dot_general(forces, weights[p], (((1,), (1,)), ((), ())), preferred_element_type=f32)
        both = both[:, :CELLS] + both[:, CELLS:]
        for i in range(2):
            part = both[8 * i : 8 * i + 8, :]
            part = scale * (part + pltpu.roll(part, 4, 0))
            r = row_of[0, 2 * p + i] + first
            for k in range(VARS):
                out[k, pl.ds(r, 1), :] = out[k, pl.ds(r, 1), :] + part[k : k + 1, :]


def first_kernel(
    got, waves, state, flow, weights, goals, rates, row_list, partial, down, up, packs,
    one, samples, row_of, sem,
):
    slots = got.shape[0]
    rows = state.shape[1]
    named = jnp.where(
        lax.broadcasted_iota(jnp.int32, (slots, CELLS), 0) == lanes_of(slots), got[:, 3, :], 0.0
    )
    row_list[...] = jnp.broadcast_to(jnp.sum(named, 0, keepdims=True).astype(jnp.int32), (8, CELLS))
    copy = pltpu.make_async_copy(row_list, row_of, sem)
    copy.start()
    middle = lax.broadcasted_iota(jnp.int32, (CELLS, CELLS), 0).astype(f32) + 0.5

    def build(p, carry):
        for i in range(2):
            t = 2 * p + i
            gap = middle - got[t, 0:1, :]
            weight = jnp.exp2(gap * gap * got[t, 1:2, :])
            whole = 1.0 / jnp.sum(weight, 0, keepdims=True)
            high = weight.astype(bf16)
            weights[p, 0:CELLS, CELLS * i : CELLS * (i + 1)] = high
            weights[p, CELLS : 2 * CELLS, CELLS * i : CELLS * (i + 1)] = (weight - high.astype(f32)).astype(bf16)
            scaled = got[t, 2:3, :] * whole
            target = got[t, 4:8, :]
            goals[t] = jnp.concatenate([target, target], 0) * scaled
            rates[t] = jnp.broadcast_to(scaled * whole, (8, CELLS))
        return carry

    lax.fori_loop(0, slots // 2, build, 0)
    one[...] = waves[...]
    copy.wait()
    sample(state, 0, row_of, samples)
    add_sources(samples, weights, goals, rates, row_of, one, TOP, time_step)
    sample(one, TOP, row_of, samples)
    for r0 in range(0, rows, CHUNK):
        change = chunk_rates(one, flow, None, r0, 0, 0)
        for k in range(VARS):
            partial[k, TOP + r0 : TOP + r0 + CHUNK, :] = (
                0.75 * state[k, r0 : r0 + CHUNK, :]
                + 0.25 * one[k, TOP + r0 : TOP + r0 + CHUNK, :]
                + quarter * change[k]
            )
    fill_rows(partial, [jnp.zeros((1, CELLS), f32)] * VARS, [jnp.zeros((1, CELLS), f32)] * VARS)
    add_sources(samples, weights, goals, rates, row_of, partial, TOP, quarter)
    for out, r in ((up, 0), (down, rows - 1)):
        for k in range(VARS):
            out[k : k + 1, :] = one[k, TOP + r : TOP + r + 1, :]
            out[4 + k : 5 + k, :] = partial[k, TOP + r : TOP + r + 1, :]
    columns = []
    for lane in (0, CELLS - 1):
        columns += edge_columns(one, TOP, lane) + edge_columns(partial, TOP, lane)
    packs[...] = turned(columns)[0:32, :]


def across_rows(beside, flow_row, side):
    along = [beside[k : k + 1, :] for k in range(VARS)]
    factor = -side * eighth
    return [
        factor * (flow_row * along[0] + along[1]),
        factor * (flow_row * along[1] + along[3]),
        factor * (flow_row * along[2]),
        factor * (flow_row * along[3] + along[1]),
    ]


def columns_kernel(above, below, flow, packs, right, left):
    rows = flow.shape[0]
    last = rows // CELLS - 1
    lane = lanes_of(1)
    from_above = across_rows(above, flow[0:1, :], -1)
    from_below = across_rows(below, flow[rows - 1 : rows, :], 1)
    for out, start, at in ((left, 0, 0), (right, 16, CELLS - 1)):
        out[0:16, :] = packs[start : start + 16, :]
        for k in (2, 3):
            top, low = from_above[k], from_below[k]
            if at == 0:
                low = pltpu.roll(low, CELLS - 1, 1)
            else:
                top = pltpu.roll(top, 1, 1)
            r = 8 + 4 * (k - 2)
            out[r : r + 1, :] = out[r : r + 1, :] + jnp.where(lane == 0, top, 0.0)
            r = r + last
            out[r : r + 1, :] = out[r : r + 1, :] + jnp.where(lane == CELLS - 1, low, 0.0)
        out[16:17, :] = above[2:3, :]
        out[17:18, :] = below[2:3, :]
        out[18:19, :] = above[3:4, :]
        out[19:20, :] = below[3:4, :]
        out[20:24, :] = jnp.zeros((4, CELLS), f32)


def last_kernel(
    row_of, partial, state, flow, above, below, above_first, below_first, from_left, from_right,
    up, down, packs, weights, goals, rates, out, two, sides, samples,
):
    rows = state.shape[1]
    lane = lanes_of(1)
    own_left, own_right = packs[0:8, :], packs[16:24, :]
    halo_left = from_left[8:16, :] - eighth * jnp.concatenate([own_left[4:8, :], own_left[0:4, :]], 0)
    halo_right = from_right[8:16, :] + eighth * jnp.concatenate([own_right[4:8, :], own_right[0:4, :]], 0)
    sides[...] = jnp.concatenate(
        [from_left[0:8, :], from_right[0:8, :], halo_left, halo_right, jnp.zeros((CELLS - 32, CELLS), f32)], 0
    ).T

    def corner(west, east):
        return eighth * (
            jnp.where(lane == 0, pltpu.roll(west, 1, 1), 0.0)
            - jnp.where(lane == CELLS - 1, pltpu.roll(east, CELLS - 1, 1), 0.0)
        )

    halos = []
    for near, first, own, side, r in ((above, above_first, up, 1, 16), (below, below_first, down, -1, 17)):
        added = across_rows(own, first[4:5, :], side)
        v_term = corner(from_left[r : r + 1, :], from_right[r : r + 1, :])
        p_term = corner(from_left[r + 2 : r + 3, :], from_right[r + 2 : r + 3, :])
        turn = [v_term, 0.0, p_term, v_term]
        halos.append([first[5:6, :] * (near[4 + k : 5 + k, :] + added[k] + turn[k]) for k in range(VARS)])
    fill_rows(two, halos[0], halos[1])

    wide = lanes_of(CHUNK)
    for r0 in range(0, rows, CHUNK):
        block, within = r0 // CELLS, r0 % CELLS

        def beside(place):
            west = sides[within : within + CHUNK, place : place + 1]
            east = sides[within : within + CHUNK, 8 + place : 9 + place]
            return eighth * (jnp.where(wide == 0, west, 0.0) - jnp.where(wide == CELLS - 1, east, 0.0))

        v_term, p_term = beside(block), beside(4 + block)
        here = slice(TOP + r0, TOP + r0 + CHUNK)
        two[0, here, :] = partial[0, here, :] + v_term
        two[1, here, :] = partial[1, here, :]
        two[2, here, :] = partial[2, here, :] + p_term
        two[3, here, :] = partial[3, here, :] + v_term
    for near, r, side in ((above, 0, -1), (below, rows - 1, 1)):
        added = across_rows(near, flow[r : r + 1, :], side)
        for k in range(VARS):
            two[k, TOP + r : TOP + r + 1, :] = two[k, TOP + r : TOP + r + 1, :] + added[k]

    sample(two, TOP, row_of, samples)
    for r0 in range(0, rows, CHUNK):
        change = chunk_rates(two, flow, sides, r0, 16, 24)
        for k in range(VARS):
            out[k, r0 : r0 + CHUNK, :] = state[k, r0 : r0 + CHUNK, :] / 3.0 + (2.0 / 3.0) * (
                two[k, TOP + r0 : TOP + r0 + CHUNK, :] + time_step * change[k]
            )
    add_sources(samples, weights, goals, rates, row_of, out, 0, (2.0 / 3.0) * time_step)


def to_neighbours(forward, back, axis, closed):
    count = lax.axis_size(axis)
    ends = count if closed else count - 1
    return (
        lax.ppermute(forward, axis, [(i, (i + 1) % count) for i in range(ends)]),
        lax.ppermute(back, axis, [((i + 1) % count, i) for i in range(ends)]),
    )


def per_device(
    gas_state,
    mean_flow,
    part_target,
    part_offset,
    part_width,
    part_rate,
    cell_index,
    dest_owner,
    gas_row,
    live_count,
):
    sectors = lax.axis_size("azim")
    tiles = cell_index.shape[0]
    rows = gas_state.shape[1]
    slots = sectors * CAP
    pairs = slots // 2
    padded = (VARS, rows + 2 * TOP, CELLS)
    params = pltpu.CompilerParams(vmem_limit_bytes=VMEM_BYTES)
    edge = shape((8, CELLS))

    send = pl.pallas_call(
        slots_kernel,
        out_shape=shape((slots, 8, CELLS)),
        in_specs=[smem()] * 3 + [vmem()] * 5,
        out_specs=vmem(),
        scratch_shapes=[pltpu.VMEM((tiles, CELLS), f32)] * 3 + [pltpu.SMEM((sectors,), jnp.int32)],
        name="slots",
    )(dest_owner[:, 0], gas_row, live_count, part_target, part_offset, part_width, part_rate, cell_index)
    got = lax.all_to_all(send, "azim", split_axis=0, concat_axis=0, tiled=True)

    down, up, right, left = pl.pallas_call(
        edges_kernel,
        out_shape=[edge] * 4,
        in_specs=[vmem()] * 2,
        out_specs=[vmem()] * 4,
        name="edges",
    )(gas_state, mean_flow)
    above_first, below_first = to_neighbours(down, up, "axial", False)
    from_left, from_right = to_neighbours(right, left, "azim", True)
    waves = pl.pallas_call(
        waves_kernel,
        out_shape=shape(padded),
        in_specs=[vmem()] * 6,
        out_specs=vmem(),
        scratch_shapes=[pltpu.VMEM(padded, f32), pltpu.VMEM((CELLS, CELLS), f32)],
        compiler_params=params,
        name="waves",
    )(gas_state, mean_flow, above_first, below_first, from_left, from_right)

    weights, goals, rates, row_list, partial, down, up, packs = pl.pallas_call(
        first_kernel,
        out_shape=[
            shape((pairs, 2 * CELLS, 2 * CELLS), bf16),
            shape((slots, 8, CELLS)),
            shape((slots, 8, CELLS)),
            shape((8, CELLS), jnp.int32),
            shape(padded),
            edge,
            edge,
            shape((32, CELLS)),
        ],
        in_specs=[vmem()] * 4,
        out_specs=[vmem()] * 8,
        scratch_shapes=[
            pltpu.VMEM(padded, f32),
            pltpu.VMEM((slots * 8, CELLS), f32),
            pltpu.SMEM((8, CELLS), jnp.int32),
            pltpu.SemaphoreType.DMA,
        ],
        compiler_params=params,
        name="first",
    )(got, waves, gas_state, mean_flow)
    above, below = to_neighbours(down, up, "axial", False)
    right, left = pl.pallas_call(
        columns_kernel,
        out_shape=[shape((24, CELLS))] * 2,
        in_specs=[vmem()] * 4,
        out_specs=[vmem()] * 2,
        name="columns",
    )(above, below, mean_flow, packs)
    from_left, from_right = to_neighbours(right, left, "azim", True)
    return pl.pallas_call(
        last_kernel,
        out_shape=shape(gas_state.shape),
        in_specs=[smem()] + [vmem()] * 15,
        out_specs=vmem(),
        scratch_shapes=[
            pltpu.VMEM(padded, f32),
            pltpu.VMEM((CELLS, CELLS), f32),
            pltpu.VMEM((slots * 8, CELLS), f32),
        ],
        compiler_params=params,
        name="last",
    )(
        row_list, partial, gas_state, mean_flow, above, below, above_first, below_first, from_left, from_right,
        up, down, packs, weights, goals, rates,
    )


def solution(mesh):
    placed = (
        P(None, "axial", "azim"),
        P("axial", "azim"),
        P(("axial", "azim"), None, None),
        P(("axial", "azim"), None),
        P(("axial", "azim"), None),
        P(("axial", "azim"), None),
        P(("axial", "azim"), None),
        P(("axial", "azim"), None),
        P(("axial", "azim")),
        P(("axial", "azim")),
    )
    return jax.shard_map(
        per_device, mesh=mesh, in_specs=placed, out_specs=P(None, "axial", "azim"), check_vma=False
    )
```

```python
import math

import jax
import jax.numpy as jnp
from jax import lax
from jax.experimental import pallas as pl
from jax.experimental.pallas import tpu as pltpu
from jax.sharding import PartitionSpec as P

CAP = 2
CELLS = 128
VARS = 4
TOP = 8
CHUNK = 32
MIB = 1024 * 1024

time_step = 0.8
quarter = 0.25 * time_step
eighth = 0.125 * time_step

f32 = jnp.float32
bf16 = jnp.bfloat16


def vmem():
    return pl.BlockSpec(memory_space=pltpu.VMEM)


def smem():
    return pl.BlockSpec(memory_space=pltpu.SMEM)


def room(mib):
    return pltpu.CompilerParams(vmem_limit_bytes=mib * MIB)


def shape(dims, dtype=f32):
    return jax.ShapeDtypeStruct(dims, dtype)


def lanes_of(rows):
    return lax.broadcasted_iota(jnp.int32, (rows, CELLS), 1)


def slots_kernel(dest, gas_row, live, target, offset, width, rate, cell, send, centre_of, factor_of, live_of, used):
    tiles = offset.shape[0]
    sectors = send.shape[0] // CAP
    send[...] = jnp.zeros(send.shape, f32)
    centre_of[...] = cell[...].astype(f32) + offset[...]
    factor_of[...] = (-0.5 / math.log(2.0)) / (width[...] * width[...])
    particle = lax.broadcasted_iota(jnp.int32, (tiles, CELLS), 0) * CELLS + lanes_of(tiles)
    live_of[...] = jnp.where(particle < live[0], rate[...], 0.0)
    for s in range(sectors):
        used[s] = 0
    for t in range(tiles):
        sector = dest[t]
        earlier = used[sector]
        used[sector] = earlier + 1
        slot = sector * CAP + earlier
        send[slot, 0:1, :] = centre_of[t : t + 1, :]
        send[slot, 1:2, :] = factor_of[t : t + 1, :]
        send[slot, 2:3, :] = live_of[t : t + 1, :]
        send[slot, 3:4, :] = jnp.full((1, CELLS), gas_row[t].astype(f32))
        send[slot, 4:8, :] = target[t]


def turned(columns):
    lane = lanes_of(CELLS)
    total = jnp.zeros((CELLS, CELLS), f32)
    for i, column in enumerate(columns):
        total = jnp.where(lane == i, column, total)
    return total.T


def edge_columns(cells, first, lane):
    blocks = (cells.shape[1] - 2 * first) // CELLS
    return [
        cells[k, first + CELLS * b : first + CELLS * (b + 1), lane : lane + 1] for k in (2, 3) for b in range(blocks)
    ]


def by_pair(first, second):
    even = lax.axis_index("axial") % 2 == 0
    return jnp.where(even, first, second), jnp.where(even, second, first)


def edges_kernel(state, flow, near, far, right, left):
    rows = state.shape[1]
    ends = []
    for r in (0, rows - 1):
        lines = [state[k, r : r + 1, :] for k in range(VARS)] + [flow[r : r + 1, :], jnp.ones((3, CELLS), f32)]
        ends.append(jnp.concatenate(lines, 0))
    near[...], far[...] = by_pair(ends[1], ends[0])
    both = turned(edge_columns(state, 0, 0) + edge_columns(state, 0, CELLS - 1))
    left[...] = both[0:8, :]
    right[...] = both[8:16, :]


def chunk_rates(cells, flow, sides, r0, left_at, right_at):
    lane = lanes_of(CHUNK)
    here = slice(TOP + r0, TOP + r0 + CHUNK)
    dx = [
        0.5 * (cells[k, TOP + r0 + 1 : TOP + r0 + CHUNK + 1, :] - cells[k, TOP + r0 - 1 : TOP + r0 + CHUNK - 1, :])
        for k in range(VARS)
    ]
    dy = []
    block, within = r0 // CELLS, r0 % CELLS
    for k in (2, 3):
        cell = cells[k, here, :]
        if sides is None:
            before, after = 0.0, 0.0
        else:
            place = 4 * (k - 2) + block
            before = sides[within : within + CHUNK, left_at + place : left_at + place + 1]
            after = sides[within : within + CHUNK, right_at + place : right_at + place + 1]
        west = jnp.where(lane == 0, before, pltpu.roll(cell, 1, 1))
        east = jnp.where(lane == CELLS - 1, after, pltpu.roll(cell, CELLS - 1, 1))
        dy.append(0.5 * (east - west))
    speed = flow[r0 : r0 + CHUNK, :]
    spread = dx[1] + dy[0]
    return [
        -speed * dx[0] - spread,
        -speed * dx[1] - dx[3],
        -speed * dx[2] - dy[1],
        -speed * dx[3] - spread,
    ]


def fill_rows(cells, top, bottom):
    rows = cells.shape[1] - 2 * TOP
    for k in range(VARS):
        cells[k, TOP - 1 : TOP, :] = top[k]
        cells[k, TOP + rows : TOP + rows + 1, :] = bottom[k]


def waves_kernel(state, flow, near, far, from_left, from_right, out, padded, sides):
    rows = state.shape[1]
    below, above = by_pair(near[...], far[...])
    padded[:, TOP : TOP + rows, :] = state[...]
    fill_rows(padded, [above[k : k + 1, :] for k in range(VARS)], [below[k : k + 1, :] for k in range(VARS)])
    sides[...] = jnp.concatenate([from_left[...], from_right[...], jnp.zeros((CELLS - 16, CELLS), f32)], 0).T
    for r0 in range(0, rows, CHUNK):
        rates = chunk_rates(padded, flow, sides, r0, 0, 8)
        for k in range(VARS):
            out[k, TOP + r0 : TOP + r0 + CHUNK, :] = state[k, r0 : r0 + CHUNK, :] + time_step * rates[k]
    fill_rows(out, [jnp.zeros((1, CELLS), f32)] * VARS, [jnp.zeros((1, CELLS), f32)] * VARS)


def sample(cells, first, row_of, samples):
    for t in range(samples.shape[0] // 8):
        r = row_of[0, t] + first
        for k in range(VARS):
            line = cells[k, pl.ds(r, 1), :]
            samples[8 * t + k : 8 * t + k + 1, :] = line
            samples[8 * t + 4 + k : 8 * t + 5 + k, :] = line


def high_and_low(values):
    high = values.astype(bf16).astype(f32)
    low_row = lax.broadcasted_iota(jnp.int32, values.shape, 0) % 8 >= 4
    return jnp.where(low_row, values - high, high)


def seen_by(samples, weights, p):
    seen = high_and_low(samples[16 * p : 16 * p + 16, :]).astype(bf16)
    sums = jnp.dot(jnp.concatenate([seen, seen], 1), weights[p], preferred_element_type=f32)
    parts = [sums[8 * i : 8 * i + 8, CELLS * i : CELLS * (i + 1)] for i in range(2)]
    return [part + pltpu.roll(part, 4, 0) for part in parts]


def add_pair(samples, weights, goals, rates, row_of, out, first, scale, p):
    nothing = jnp.zeros((8, CELLS), f32)
    sums = seen_by(samples, weights, p)
    forces = [high_and_low(goals[2 * p + i] - rates[2 * p + i] * sums[i]) for i in range(2)]
    forces = jnp.concatenate(
        [jnp.concatenate([forces[0], nothing], 1), jnp.concatenate([nothing, forces[1]], 1)], 0
    ).astype(bf16)
    both = lax.dot_general(forces, weights[p], (((1,), (1,)), ((), ())), preferred_element_type=f32)
    both = both[:, :CELLS] + both[:, CELLS:]
    for i in range(2):
        part = both[8 * i : 8 * i + 8, :]
        part = scale * (part + pltpu.roll(part, 4, 0))
        r = row_of[0, 2 * p + i] + first
        for k in range(VARS):
            out[k, pl.ds(r, 1), :] = out[k, pl.ds(r, 1), :] + part[k : k + 1, :]


def add_sources(samples, weights, goals, rates, row_of, out, first, scale):
    for p in range(weights.shape[0]):
        add_pair(samples, weights, goals, rates, row_of, out, first, scale, p)


def build_pair(got, weights, goals, rates, p):
    middle = lax.broadcasted_iota(jnp.int32, (CELLS, CELLS), 0).astype(f32) + 0.5
    for i in range(2):
        t = 2 * p + i
        gap = middle - got[t, 0:1, :]
        weight = jnp.exp2(gap * gap * got[t, 1:2, :])
        whole = 1.0 / jnp.sum(weight, 0, keepdims=True)
        high = weight.astype(bf16)
        weights[p, 0:CELLS, CELLS * i : CELLS * (i + 1)] = high
        weights[p, CELLS : 2 * CELLS, CELLS * i : CELLS * (i + 1)] = (weight - high.astype(f32)).astype(bf16)
        scaled = got[t, 2:3, :] * whole
        target = got[t, 4:8, :]
        goals[t] = jnp.concatenate([target, target], 0) * scaled
        rates[t] = jnp.broadcast_to(scaled * whole, (8, CELLS))


def first_kernel(
    got, waves, state, flow, weights, goals, rates, row_list, partial, near, far, packs,
    one, samples, row_of, sem,
):
    slots = got.shape[0]
    rows = state.shape[1]
    named = jnp.where(
        lax.broadcasted_iota(jnp.int32, (slots, CELLS), 0) == lanes_of(slots), got[:, 3, :], 0.0
    )
    row_list[...] = jnp.broadcast_to(jnp.sum(named, 0, keepdims=True).astype(jnp.int32), (8, CELLS))
    copy = pltpu.make_async_copy(row_list, row_of, sem)
    copy.start()
    one[...] = waves[...]
    copy.wait()
    sample(state, 0, row_of, samples)
    for p in range(slots // 2):
        build_pair(got, weights, goals, rates, p)
        add_pair(samples, weights, goals, rates, row_of, one, TOP, time_step, p)
    sample(one, TOP, row_of, samples)
    for r0 in range(0, rows, CHUNK):
        change = chunk_rates(one, flow, None, r0, 0, 0)
        for k in range(VARS):
            partial[k, TOP + r0 : TOP + r0 + CHUNK, :] = (
                0.75 * state[k, r0 : r0 + CHUNK, :]
                + 0.25 * one[k, TOP + r0 : TOP + r0 + CHUNK, :]
                + quarter * change[k]
            )
    fill_rows(partial, [jnp.zeros((1, CELLS), f32)] * VARS, [jnp.zeros((1, CELLS), f32)] * VARS)
    add_sources(samples, weights, goals, rates, row_of, partial, TOP, quarter)
    ends = []
    for r in (TOP, TOP + rows - 1):
        ends.append(jnp.concatenate([cells[k, r : r + 1, :] for cells in (one, partial) for k in range(VARS)], 0))
    near[...], far[...] = by_pair(ends[1], ends[0])
    columns = []
    for lane in (0, CELLS - 1):
        columns += edge_columns(one, TOP, lane) + edge_columns(partial, TOP, lane)
    packs[...] = turned(columns)[0:32, :]


def across_rows(beside, flow_row, side):
    along = [beside[k : k + 1, :] for k in range(VARS)]
    factor = -side * eighth
    return [
        factor * (flow_row * along[0] + along[1]),
        factor * (flow_row * along[1] + along[3]),
        factor * (flow_row * along[2]),
        factor * (flow_row * along[3] + along[1]),
    ]


def columns_kernel(near, far, flow, packs, right, left):
    rows = flow.shape[0]
    below, above = by_pair(near[...], far[...])
    last = rows // CELLS - 1
    lane = lanes_of(1)
    from_above = across_rows(above, flow[0:1, :], -1)
    from_below = across_rows(below, flow[rows - 1 : rows, :], 1)
    for out, start, at in ((left, 0, 0), (right, 16, CELLS - 1)):
        out[0:16, :] = packs[start : start + 16, :]
        for k in (2, 3):
            top, low = from_above[k], from_below[k]
            if at == 0:
                low = pltpu.roll(low, CELLS - 1, 1)
            else:
                top = pltpu.roll(top, 1, 1)
            r = 8 + 4 * (k - 2)
            out[r : r + 1, :] = out[r : r + 1, :] + jnp.where(lane == 0, top, 0.0)
            r = r + last
            out[r : r + 1, :] = out[r : r + 1, :] + jnp.where(lane == CELLS - 1, low, 0.0)
        out[16:17, :] = above[2:3, :]
        out[17:18, :] = below[2:3, :]
        out[18:19, :] = above[3:4, :]
        out[19:20, :] = below[3:4, :]
        out[20:24, :] = jnp.zeros((4, CELLS), f32)


def last_kernel(
    row_of, partial, state, flow, near, far, near_first, far_first, from_left, from_right,
    own_near, own_far, packs, weights, goals, rates, out, two, sides, samples,
):
    rows = state.shape[1]
    lane = lanes_of(1)
    below, above = by_pair(near[...], far[...])
    below_first, above_first = by_pair(near_first[...], far_first[...])
    down, up = by_pair(own_near[...], own_far[...])
    own_left, own_right = packs[0:8, :], packs[16:24, :]
    halo_left = from_left[8:16, :] - eighth * jnp.concatenate([own_left[4:8, :], own_left[0:4, :]], 0)
    halo_right = from_right[8:16, :] + eighth * jnp.concatenate([own_right[4:8, :], own_right[0:4, :]], 0)
    sides[...] = jnp.concatenate(
        [from_left[0:8, :], from_right[0:8, :], halo_left, halo_right, jnp.zeros((CELLS - 32, CELLS), f32)], 0
    ).T

    def corner(west, east):
        return eighth * (
            jnp.where(lane == 0, pltpu.roll(west, 1, 1), 0.0)
            - jnp.where(lane == CELLS - 1, pltpu.roll(east, CELLS - 1, 1), 0.0)
        )

    halos = []
    for near, first, own, side, r in ((above, above_first, up, 1, 16), (below, below_first, down, -1, 17)):
        added = across_rows(own, first[4:5, :], side)
        v_term = corner(from_left[r : r + 1, :], from_right[r : r + 1, :])
        p_term = corner(from_left[r + 2 : r + 3, :], from_right[r + 2 : r + 3, :])
        turn = [v_term, 0.0, p_term, v_term]
        halos.append([first[5:6, :] * (near[4 + k : 5 + k, :] + added[k] + turn[k]) for k in range(VARS)])
    fill_rows(two, halos[0], halos[1])

    wide = lanes_of(CHUNK)
    for r0 in range(0, rows, CHUNK):
        block, within = r0 // CELLS, r0 % CELLS

        def beside(place):
            west = sides[within : within + CHUNK, place : place + 1]
            east = sides[within : within + CHUNK, 8 + place : 9 + place]
            return eighth * (jnp.where(wide == 0, west, 0.0) - jnp.where(wide == CELLS - 1, east, 0.0))

        v_term, p_term = beside(block), beside(4 + block)
        here = slice(TOP + r0, TOP + r0 + CHUNK)
        two[0, here, :] = partial[0, here, :] + v_term
        two[1, here, :] = partial[1, here, :]
        two[2, here, :] = partial[2, here, :] + p_term
        two[3, here, :] = partial[3, here, :] + v_term
    for near, r, side in ((above, 0, -1), (below, rows - 1, 1)):
        added = across_rows(near, flow[r : r + 1, :], side)
        for k in range(VARS):
            two[k, TOP + r : TOP + r + 1, :] = two[k, TOP + r : TOP + r + 1, :] + added[k]

    sample(two, TOP, row_of, samples)
    for r0 in range(0, rows, CHUNK):
        change = chunk_rates(two, flow, sides, r0, 16, 24)
        for k in range(VARS):
            out[k, r0 : r0 + CHUNK, :] = state[k, r0 : r0 + CHUNK, :] / 3.0 + (2.0 / 3.0) * (
                two[k, TOP + r0 : TOP + r0 + CHUNK, :] + time_step * change[k]
            )
    add_sources(samples, weights, goals, rates, row_of, out, 0, (2.0 / 3.0) * time_step)


def to_axial(near, far):
    count = lax.axis_size("axial")

    def pairs(start):
        return [move for i in range(start, count - 1, 2) for move in ((i, i + 1), (i + 1, i))]

    return lax.ppermute(near, "axial", pairs(0)), lax.ppermute(far, "axial", pairs(1))


def to_azimuthal(right, left):
    count = lax.axis_size("azim")
    return (
        lax.ppermute(right, "azim", [(i, (i + 1) % count) for i in range(count)]),
        lax.ppermute(left, "azim", [((i + 1) % count, i) for i in range(count)]),
    )


def per_device(
    gas_state,
    mean_flow,
    part_target,
    part_offset,
    part_width,
    part_rate,
    cell_index,
    dest_owner,
    gas_row,
    live_count,
):
    sectors = lax.axis_size("azim")
    tiles = cell_index.shape[0]
    rows = gas_state.shape[1]
    slots = sectors * CAP
    pairs = slots // 2
    padded = (VARS, rows + 2 * TOP, CELLS)
    edge = shape((8, CELLS))

    send = pl.pallas_call(
        slots_kernel,
        out_shape=shape((slots, 8, CELLS)),
        in_specs=[smem()] * 3 + [vmem()] * 5,
        out_specs=vmem(),
        scratch_shapes=[pltpu.VMEM((tiles, CELLS), f32)] * 3 + [pltpu.SMEM((sectors,), jnp.int32)],
        name="slots",
    )(dest_owner[:, 0], gas_row, live_count, part_target, part_offset, part_width, part_rate, cell_index)
    got = lax.all_to_all(send, "azim", split_axis=0, concat_axis=0, tiled=True)

    near, far, right, left = pl.pallas_call(
        edges_kernel,
        out_shape=[edge] * 4,
        in_specs=[vmem()] * 2,
        out_specs=[vmem()] * 4,
        name="edges",
    )(gas_state, mean_flow)
    near_first, far_first = to_axial(near, far)
    from_left, from_right = to_azimuthal(right, left)
    waves = pl.pallas_call(
        waves_kernel,
        out_shape=shape(padded),
        in_specs=[vmem()] * 6,
        out_specs=vmem(),
        scratch_shapes=[pltpu.VMEM(padded, f32), pltpu.VMEM((CELLS, CELLS), f32)],
        compiler_params=room(8),
        name="waves",
    )(gas_state, mean_flow, near_first, far_first, from_left, from_right)

    weights, goals, rates, row_list, partial, own_near, own_far, packs = pl.pallas_call(
        first_kernel,
        out_shape=[
            shape((pairs, 2 * CELLS, 2 * CELLS), bf16),
            shape((slots, 8, CELLS)),
            shape((slots, 8, CELLS)),
            shape((8, CELLS), jnp.int32),
            shape(padded),
            edge,
            edge,
            shape((32, CELLS)),
        ],
        in_specs=[vmem()] * 4,
        out_specs=[vmem()] * 8,
        scratch_shapes=[
            pltpu.VMEM(padded, f32),
            pltpu.VMEM((slots * 8, CELLS), f32),
            pltpu.SMEM((8, CELLS), jnp.int32),
            pltpu.SemaphoreType.DMA,
        ],
        compiler_params=room(16),
        name="first",
    )(got, waves, gas_state, mean_flow)
    near, far = to_axial(own_near, own_far)
    right, left = pl.pallas_call(
        columns_kernel,
        out_shape=[shape((24, CELLS))] * 2,
        in_specs=[vmem()] * 4,
        out_specs=[vmem()] * 2,
        compiler_params=room(2),
        name="columns",
    )(near, far, mean_flow, packs)
    from_left, from_right = to_azimuthal(right, left)
    return pl.pallas_call(
        last_kernel,
        out_shape=shape(gas_state.shape),
        in_specs=[smem()] + [vmem()] * 15,
        out_specs=vmem(),
        scratch_shapes=[
            pltpu.VMEM(padded, f32),
            pltpu.VMEM((CELLS, CELLS), f32),
            pltpu.VMEM((slots * 8, CELLS), f32),
        ],
        compiler_params=room(16),
        name="last",
    )(
        row_list, partial, gas_state, mean_flow, near, far, near_first, far_first, from_left, from_right,
        own_near, own_far, packs, weights, goals, rates,
    )


def solution(mesh):
    placed = (
        P(None, "axial", "azim"),
        P("axial", "azim"),
        P(("axial", "azim"), None, None),
        P(("axial", "azim"), None),
        P(("axial", "azim"), None),
        P(("axial", "azim"), None),
        P(("axial", "azim"), None),
        P(("axial", "azim"), None),
        P(("axial", "azim")),
        P(("axial", "azim")),
    )
    return jax.shard_map(
        per_device, mesh=mesh, in_specs=placed, out_specs=P(None, "axial", "azim"), check_vma=False
    )
```

```python
import functools
import math

import jax
import jax.numpy as jnp
from jax import lax
from jax.experimental import pallas as pl
from jax.experimental.pallas import tpu as pltpu
from jax.sharding import PartitionSpec as P

CAP = 2
CELLS = 128
VARS = 4
TOP = 8
CHUNK = 32
EACH = 7
LINES = CAP * EACH + 1
MIB = 1024 * 1024

time_step = 0.8
quarter = 0.25 * time_step
eighth = 0.125 * time_step

f32 = jnp.float32
bf16 = jnp.bfloat16


def vmem():
    return pl.BlockSpec(memory_space=pltpu.VMEM)


def smem():
    return pl.BlockSpec(memory_space=pltpu.SMEM)


def room(mib):
    return pltpu.CompilerParams(vmem_limit_bytes=mib * MIB)


def shape(dims, dtype=f32):
    return jax.ShapeDtypeStruct(dims, dtype)


def lanes_of(rows):
    return lax.broadcasted_iota(jnp.int32, (rows, CELLS), 1)


def slots_kernel(dest, gas_row, live, target, offset, width, rate, cell, send, centre_of, factor_of, live_of, latest):
    tiles = offset.shape[0]
    for t in range(tiles):
        latest[dest[t]] = t
    send[...] = jnp.zeros(send.shape, f32)
    centre_of[...] = cell[...].astype(f32) + offset[...]
    factor_of[...] = (-0.5 / math.log(2.0)) / (width[...] * width[...])
    particle = lax.broadcasted_iota(jnp.int32, (tiles, CELLS), 0) * CELLS + lanes_of(tiles)
    live_of[...] = jnp.where(particle < live[0], rate[...], 0.0)
    turn = lanes_of(1) % CAP
    for t in range(tiles):
        slot = (latest[dest[t]] == t).astype(jnp.int32)
        first = dest[t] * LINES
        at = first + slot * EACH
        send[pl.ds(at, 1), :] = centre_of[t : t + 1, :]
        send[pl.ds(at + 1, 1), :] = factor_of[t : t + 1, :]
        send[pl.ds(at + 2, 1), :] = live_of[t : t + 1, :]
        send[pl.ds(at + 3, 4), :] = target[t]
        row_line = pl.ds(first + CAP * EACH, 1)
        send[row_line, :] = jnp.where(turn == slot, gas_row[t].astype(f32), send[row_line, :])


def turned(columns):
    lane = lanes_of(CELLS)
    total = jnp.zeros((CELLS, CELLS), f32)
    for i, column in enumerate(columns):
        total = jnp.where(lane == i, column, total)
    return total.T


def edge_columns(cells, first, lane):
    height = cells.shape[0] // VARS
    starts = [k * height + first + CELLS * b for k in (2, 3) for b in range((height - 2 * first) // CELLS)]
    return [cells[at : at + CELLS, lane : lane + 1] for at in starts]


def by_pair(first, second):
    even = lax.axis_index("axial") % 2 == 0
    return jnp.where(even, first, second), jnp.where(even, second, first)


def edges_kernel(state, flow, near, far, right, left):
    rows = flow.shape[0]
    ends = []
    for r in (0, rows - 1):
        lines = [state[k * rows + r : k * rows + r + 1, :] for k in range(VARS)]
        lines += [flow[r : r + 1, :], jnp.ones((3, CELLS), f32)]
        ends.append(jnp.concatenate(lines, 0))
    near[...], far[...] = by_pair(ends[1], ends[0])
    both = turned(edge_columns(state, 0, 0) + edge_columns(state, 0, CELLS - 1))
    left[...] = both[0:8, :]
    right[...] = both[8:16, :]


def chunk_rates(cells, flow, sides, r0, left_at, right_at):
    lane = lanes_of(CHUNK)
    starts = [k * (flow.shape[0] + 2 * TOP) + TOP + r0 for k in range(VARS)]
    dx = [0.5 * (cells[at + 1 : at + CHUNK + 1, :] - cells[at - 1 : at + CHUNK - 1, :]) for at in starts]
    dy = []
    block, within = r0 // CELLS, r0 % CELLS
    for k in (2, 3):
        cell = cells[starts[k] : starts[k] + CHUNK, :]
        if sides is None:
            before, after = 0.0, 0.0
        else:
            place = 4 * (k - 2) + block
            before = sides[within : within + CHUNK, left_at + place : left_at + place + 1]
            after = sides[within : within + CHUNK, right_at + place : right_at + place + 1]
        west = jnp.where(lane == 0, before, pltpu.roll(cell, 1, 1))
        east = jnp.where(lane == CELLS - 1, after, pltpu.roll(cell, CELLS - 1, 1))
        dy.append(0.5 * (east - west))
    speed = flow[r0 : r0 + CHUNK, :]
    spread = dx[1] + dy[0]
    return [
        -speed * dx[0] - spread,
        -speed * dx[1] - dx[3],
        -speed * dx[2] - dy[1],
        -speed * dx[3] - spread,
    ]


def at_row(k, r, rows):
    return k * (rows + 2 * TOP) + TOP + r


def fill_rows(cells, top, bottom):
    height = cells.shape[0] // VARS
    for k in range(VARS):
        cells[k * height + TOP - 1 : k * height + TOP, :] = top[k]
        cells[(k + 1) * height - TOP : (k + 1) * height - TOP + 1, :] = bottom[k]


def waves_kernel(state, flow, near, far, from_left, from_right, out, padded, sides):
    rows = flow.shape[0]
    below, above = by_pair(near[...], far[...])
    for k in range(VARS):
        padded[at_row(k, 0, rows) : at_row(k, rows, rows), :] = state[k * rows : (k + 1) * rows, :]
    fill_rows(padded, [above[k : k + 1, :] for k in range(VARS)], [below[k : k + 1, :] for k in range(VARS)])
    sides[...] = jnp.concatenate([from_left[...], from_right[...], jnp.zeros((CELLS - 16, CELLS), f32)], 0).T
    for r0 in range(0, rows, CHUNK):
        rates = chunk_rates(padded, flow, sides, r0, 0, 8)
        for k in range(VARS):
            here = state[k * rows + r0 : k * rows + r0 + CHUNK, :]
            out[at_row(k, r0, rows) : at_row(k, r0 + CHUNK, rows), :] = here + time_step * rates[k]
    fill_rows(out, [jnp.zeros((1, CELLS), f32)] * VARS, [jnp.zeros((1, CELLS), f32)] * VARS)


def sample(cells, first, row_of, samples):
    for t in range(samples.shape[0] // 8):
        lines = cells[pl.ds(row_of[0, t] + first, VARS, cells.shape[0] // VARS), :]
        samples[8 * t : 8 * t + 4, :] = lines
        samples[8 * t + 4 : 8 * t + 8, :] = lines


def high_and_low(values):
    high = values.astype(bf16).astype(f32)
    low_row = lax.broadcasted_iota(jnp.int32, values.shape, 0) % 8 >= 4
    return jnp.where(low_row, values - high, high)


def see_pair(samples, weights, sums, p):
    seen = high_and_low(samples[16 * p : 16 * p + 16, :]).astype(bf16)
    both = jnp.dot(jnp.concatenate([seen, seen], 1), weights[p], preferred_element_type=f32)
    for i in range(2):
        part = both[8 * i : 8 * i + 8, CELLS * i : CELLS * (i + 1)]
        sums[2 * p + i] = part + pltpu.roll(part, 4, 0)


def add_sources(sums, turned_weights, goals, rates, row_of, out, first, scale):
    nothing = jnp.zeros((8, CELLS), f32)
    for p in range(turned_weights.shape[0]):
        forces = [high_and_low(goals[t] - rates[t] * sums[t]) for t in (2 * p, 2 * p + 1)]
        forces = jnp.concatenate(
            [jnp.concatenate([forces[0], nothing], 1), jnp.concatenate([nothing, forces[1]], 1)], 0
        ).astype(bf16)
        both = jnp.dot(forces, turned_weights[p], preferred_element_type=f32)
        both = both[:, :CELLS] + both[:, CELLS:]
        for i in range(2):
            part = both[8 * i : 8 * i + 8, :]
            part = scale * (part[0:4, :] + part[4:8, :])
            lines = pl.ds(row_of[0, 2 * p + i] + first, VARS, out.shape[0] // VARS)
            out[lines, :] = out[lines, :] + part


def build_pair(got, weights, turned_weights, goals, rates, p):
    middle = lax.broadcasted_iota(jnp.int32, (CELLS, CELLS), 0).astype(f32) + 0.5
    for i in range(2):
        t = 2 * p + i
        at = p * LINES + i * EACH
        gap = middle - got[at : at + 1, :]
        weight = jnp.exp2(gap * gap * got[at + 1 : at + 2, :])
        whole = 1.0 / jnp.sum(weight, 0, keepdims=True)
        high = weight.astype(bf16)
        low = (weight - high.astype(f32)).astype(bf16)
        here = slice(CELLS * i, CELLS * (i + 1))
        weights[p, 0:CELLS, here] = high
        weights[p, CELLS : 2 * CELLS, here] = low
        turned_weights[p, here, 0:CELLS] = high.T
        turned_weights[p, here, CELLS : 2 * CELLS] = low.T
        scaled = got[at + 2 : at + 3, :] * whole
        target = got[at + 3 : at + 7, :]
        goals[t] = jnp.concatenate([target, target], 0) * scaled
        rates[t] = jnp.broadcast_to(scaled * whole, (8, CELLS))


def first_kernel(
    got, waves, state, flow, weights, turned_weights, goals, rates, row_list, partial, near, far, right, left,
    one, samples, sums, row_of, sem,
):
    pairs = got.shape[0] // LINES
    slots = CAP * pairs
    rows = flow.shape[0]
    lines = got[pl.ds(CAP * EACH, pairs, LINES), :]
    named = jnp.where(lax.broadcasted_iota(jnp.int32, (pairs, CELLS), 0) == lanes_of(pairs) // CAP, lines, 0.0)
    row_list[...] = jnp.broadcast_to(jnp.sum(named, 0, keepdims=True).astype(jnp.int32), (8, CELLS))
    copy = pltpu.make_async_copy(row_list, row_of, sem)
    copy.start()
    one[...] = waves[...]
    ahead = slots // 8
    for p in range(ahead):
        build_pair(got, weights, turned_weights, goals, rates, p)
    copy.wait()
    sample(state, 0, row_of, samples)
    for p in range(slots // 2):
        if p + ahead < slots // 2:
            build_pair(got, weights, turned_weights, goals, rates, p + ahead)
        see_pair(samples, weights, sums, p)
    add_sources(sums, turned_weights, goals, rates, row_of, one, TOP, time_step)
    sample(one, TOP, row_of, samples)
    for p in range(slots // 2):
        see_pair(samples, weights, sums, p)
    for r0 in range(0, rows, CHUNK):
        change = chunk_rates(one, flow, None, r0, 0, 0)
        for k in range(VARS):
            here = slice(at_row(k, r0, rows), at_row(k, r0 + CHUNK, rows))
            old = state[k * rows + r0 : k * rows + r0 + CHUNK, :]
            partial[here, :] = 0.75 * old + 0.25 * one[here, :] + quarter * change[k]
    fill_rows(partial, [jnp.zeros((1, CELLS), f32)] * VARS, [jnp.zeros((1, CELLS), f32)] * VARS)
    add_sources(sums, turned_weights, goals, rates, row_of, partial, TOP, quarter)
    ends = []
    for r in (0, rows - 1):
        starts = [at_row(k, r, rows) for k in range(VARS)]
        ends.append(jnp.concatenate([cells[at : at + 1, :] for cells in (one, partial) for at in starts], 0))
    near[...], far[...] = by_pair(ends[1], ends[0])
    columns = []
    for lane in (0, CELLS - 1):
        columns += edge_columns(one, TOP, lane) + edge_columns(partial, TOP, lane)
    packs = turned(columns)
    left[...] = jnp.concatenate([packs[0:16, :], jnp.zeros((8, CELLS), f32)], 0)
    right[...] = jnp.concatenate([packs[16:32, :], jnp.zeros((8, CELLS), f32)], 0)


def across_rows(beside, flow_row, side):
    along = [beside[k : k + 1, :] for k in range(VARS)]
    factor = -side * eighth
    return [
        factor * (flow_row * along[0] + along[1]),
        factor * (flow_row * along[1] + along[3]),
        factor * (flow_row * along[2]),
        factor * (flow_row * along[3] + along[1]),
    ]


def columns_kernel(is_far, beside, flow, right_so_far, left_so_far, right, left):
    rows = flow.shape[0]
    last = rows // CELLS - 1
    lane = lanes_of(1)
    message = beside[...]
    nothing = jnp.zeros_like(message)
    below, above = by_pair(nothing, message) if is_far else by_pair(message, nothing)
    from_above = across_rows(above, flow[0:1, :], -1)
    from_below = across_rows(below, flow[rows - 1 : rows, :], 1)
    for out, before, at in ((left, left_so_far, 0), (right, right_so_far, CELLS - 1)):
        out[...] = before[...]
        for k in (2, 3):
            top, low = from_above[k], from_below[k]
            if at == 0:
                low = pltpu.roll(low, CELLS - 1, 1)
            else:
                top = pltpu.roll(top, 1, 1)
            r = 8 + 4 * (k - 2)
            out[r : r + 1, :] = out[r : r + 1, :] + jnp.where(lane == 0, top, 0.0)
            r = r + last
            out[r : r + 1, :] = out[r : r + 1, :] + jnp.where(lane == CELLS - 1, low, 0.0)
        for r, line in ((16, above[2:3, :]), (17, below[2:3, :]), (18, above[3:4, :]), (19, below[3:4, :])):
            out[r : r + 1, :] = out[r : r + 1, :] + line


def last_kernel(
    row_of, partial, state, flow, near, far, near_first, far_first, from_left, from_right,
    own_near, own_far, right, left, weights, turned_weights, goals, rates, out, two, sides, samples, sums,
):
    rows = flow.shape[0]
    lane = lanes_of(1)
    below, above = by_pair(near[...], far[...])
    below_first, above_first = by_pair(near_first[...], far_first[...])
    down, up = by_pair(own_near[...], own_far[...])
    own_left, own_right = left[0:8, :], right[0:8, :]
    halo_left = from_left[8:16, :] - eighth * jnp.concatenate([own_left[4:8, :], own_left[0:4, :]], 0)
    halo_right = from_right[8:16, :] + eighth * jnp.concatenate([own_right[4:8, :], own_right[0:4, :]], 0)
    sides[...] = jnp.concatenate(
        [from_left[0:8, :], from_right[0:8, :], halo_left, halo_right, jnp.zeros((CELLS - 32, CELLS), f32)], 0
    ).T

    def corner(west, east):
        return eighth * (
            jnp.where(lane == 0, pltpu.roll(west, 1, 1), 0.0)
            - jnp.where(lane == CELLS - 1, pltpu.roll(east, CELLS - 1, 1), 0.0)
        )

    halos = []
    for near, first, own, side, r in ((above, above_first, up, 1, 16), (below, below_first, down, -1, 17)):
        added = across_rows(own, first[4:5, :], side)
        v_term = corner(from_left[r : r + 1, :], from_right[r : r + 1, :])
        p_term = corner(from_left[r + 2 : r + 3, :], from_right[r + 2 : r + 3, :])
        turn = [v_term, 0.0, p_term, v_term]
        halos.append([first[5:6, :] * (near[4 + k : 5 + k, :] + added[k] + turn[k]) for k in range(VARS)])
    fill_rows(two, halos[0], halos[1])

    wide = lanes_of(CHUNK)
    for r0 in range(0, rows, CHUNK):
        block, within = r0 // CELLS, r0 % CELLS

        def beside(place):
            west = sides[within : within + CHUNK, place : place + 1]
            east = sides[within : within + CHUNK, 8 + place : 9 + place]
            return eighth * (jnp.where(wide == 0, west, 0.0) - jnp.where(wide == CELLS - 1, east, 0.0))

        v_term, p_term = beside(block), beside(4 + block)
        for k, term in enumerate((v_term, 0.0, p_term, v_term)):
            here = slice(at_row(k, r0, rows), at_row(k, r0 + CHUNK, rows))
            two[here, :] = partial[here, :] + term
    for near, r, side in ((above, 0, -1), (below, rows - 1, 1)):
        added = across_rows(near, flow[r : r + 1, :], side)
        for k in range(VARS):
            at = at_row(k, r, rows)
            two[at : at + 1, :] = two[at : at + 1, :] + added[k]

    sample(two, TOP, row_of, samples)
    for p in range(weights.shape[0]):
        see_pair(samples, weights, sums, p)
    for r0 in range(0, rows, CHUNK):
        change = chunk_rates(two, flow, sides, r0, 16, 24)
        for k in range(VARS):
            here = slice(k * rows + r0, k * rows + r0 + CHUNK)
            now = two[at_row(k, r0, rows) : at_row(k, r0 + CHUNK, rows), :]
            out[here, :] = state[here, :] / 3.0 + (2.0 / 3.0) * (now + time_step * change[k])
    add_sources(sums, turned_weights, goals, rates, row_of, out, 0, (2.0 / 3.0) * time_step)


def to_axial(near, far):
    count = lax.axis_size("axial")

    def pairs(start):
        return [move for i in range(start, count - 1, 2) for move in ((i, i + 1), (i + 1, i))]

    far = lax.ppermute(far, "axial", pairs(1))
    return lax.ppermute(near, "axial", pairs(0)), far


def to_azimuthal(right, left):
    count = lax.axis_size("azim")
    return (
        lax.ppermute(right, "azim", [(i, (i + 1) % count) for i in range(count)]),
        lax.ppermute(left, "azim", [((i + 1) % count, i) for i in range(count)]),
    )


def per_device(
    gas_state,
    mean_flow,
    part_target,
    part_offset,
    part_width,
    part_rate,
    cell_index,
    dest_owner,
    gas_row,
    live_count,
):
    sectors = lax.axis_size("azim")
    tiles = cell_index.shape[0]
    rows = gas_state.shape[1]
    slots = sectors * CAP
    pairs = slots // 2
    padded = (VARS * (rows + 2 * TOP), CELLS)
    state = gas_state.reshape(VARS * rows, CELLS)
    edge = shape((8, CELLS))

    send = pl.pallas_call(
        slots_kernel,
        out_shape=shape((sectors * LINES, CELLS)),
        in_specs=[smem()] * 3 + [vmem()] * 5,
        out_specs=vmem(),
        scratch_shapes=[pltpu.VMEM((tiles, CELLS), f32)] * 3 + [pltpu.SMEM((sectors,), jnp.int32)],
        name="slots",
    )(dest_owner[:, 0], gas_row, live_count, part_target, part_offset, part_width, part_rate, cell_index)
    send = send.reshape(sectors, 1, LINES * CELLS)
    got = lax.all_to_all(send, "azim", split_axis=0, concat_axis=0, tiled=True).reshape(sectors * LINES, CELLS)

    near, far, right, left = pl.pallas_call(
        edges_kernel,
        out_shape=[edge] * 4,
        in_specs=[vmem()] * 2,
        out_specs=[vmem()] * 4,
        name="edges",
    )(state, mean_flow)
    near_first, far_first = to_axial(near, far)
    from_left, from_right = to_azimuthal(right, left)
    waves = pl.pallas_call(
        waves_kernel,
        out_shape=shape(padded),
        in_specs=[vmem()] * 6,
        out_specs=vmem(),
        scratch_shapes=[pltpu.VMEM(padded, f32), pltpu.VMEM((CELLS, CELLS), f32)],
        compiler_params=room(8),
        name="waves",
    )(state, mean_flow, near_first, far_first, from_left, from_right)

    weights, turned_weights, goals, rates, row_list, partial, own_near, own_far, own_right, own_left = pl.pallas_call(
        first_kernel,
        out_shape=[
            shape((pairs, 2 * CELLS, 2 * CELLS), bf16),
            shape((pairs, 2 * CELLS, 2 * CELLS), bf16),
            shape((slots, 8, CELLS)),
            shape((slots, 8, CELLS)),
            shape((8, CELLS), jnp.int32),
            shape(padded),
            edge,
            edge,
            shape((24, CELLS)),
            shape((24, CELLS)),
        ],
        in_specs=[vmem()] * 4,
        out_specs=[vmem()] * 10,
        scratch_shapes=[
            pltpu.VMEM(padded, f32),
            pltpu.VMEM((slots * 8, CELLS), f32),
            pltpu.VMEM((slots, 8, CELLS), f32),
            pltpu.SMEM((8, CELLS), jnp.int32),
            pltpu.SemaphoreType.DMA,
        ],
        compiler_params=room(15),
        name="first",
    )(got, waves, state, mean_flow)
    near, far = to_axial(own_near, own_far)
    right, left = own_right, own_left
    for is_far, beside in ((True, far), (False, near)):
        right, left = pl.pallas_call(
            functools.partial(columns_kernel, is_far),
            out_shape=[shape((24, CELLS))] * 2,
            in_specs=[vmem()] * 4,
            out_specs=[vmem()] * 2,
            compiler_params=room(2),
            name="columns",
        )(beside, mean_flow, right, left)
    from_left, from_right = to_azimuthal(right, left)
    new_state = pl.pallas_call(
        last_kernel,
        out_shape=shape(state.shape),
        in_specs=[smem()] + [vmem()] * 17,
        out_specs=vmem(),
        scratch_shapes=[
            pltpu.VMEM(padded, f32),
            pltpu.VMEM((CELLS, CELLS), f32),
            pltpu.VMEM((slots * 8, CELLS), f32),
            pltpu.VMEM((slots, 8, CELLS), f32),
        ],
        compiler_params=room(15),
        name="last",
    )(
        row_list, partial, state, mean_flow, near, far, near_first, far_first, from_left, from_right,
        own_near, own_far, own_right, own_left, weights, turned_weights, goals, rates,
    )
    return new_state.reshape(gas_state.shape)


def solution(mesh):
    placed = (
        P(None, "axial", "azim"),
        P("axial", "azim"),
        P(("axial", "azim"), None, None),
        P(("axial", "azim"), None),
        P(("axial", "azim"), None),
        P(("axial", "azim"), None),
        P(("axial", "azim"), None),
        P(("axial", "azim"), None),
        P(("axial", "azim")),
        P(("axial", "azim")),
    )
    return jax.shard_map(
        per_device, mesh=mesh, in_specs=placed, out_specs=P(None, "axial", "azim"), check_vma=False
    )
```

```python
import functools
import math

import jax
import jax.numpy as jnp
from jax import lax
from jax.experimental import pallas as pl
from jax.experimental.pallas import tpu as pltpu
from jax.sharding import PartitionSpec as P

CAP = 2
CELLS = 128
VARS = 4
TOP = 8
CHUNK = 32
EACH = 7
LINES = CAP * EACH + 1
MIB = 1024 * 1024

time_step = 0.8
quarter = 0.25 * time_step
eighth = 0.125 * time_step

f32 = jnp.float32
bf16 = jnp.bfloat16


def vmem():
    return pl.BlockSpec(memory_space=pltpu.VMEM)


def smem():
    return pl.BlockSpec(memory_space=pltpu.SMEM)


def room(mib):
    return pltpu.CompilerParams(vmem_limit_bytes=mib * MIB)


def shape(dims, dtype=f32):
    return jax.ShapeDtypeStruct(dims, dtype)


def lanes_of(rows):
    return lax.broadcasted_iota(jnp.int32, (rows, CELLS), 1)


def slots_kernel(dest, gas_row, live, target, offset, width, rate, cell, send, centre_of, factor_of, live_of, latest):
    tiles = offset.shape[0]
    for t in range(tiles):
        latest[dest[t]] = t
    send[...] = jnp.zeros(send.shape, f32)
    send[pl.ds(CAP * EACH, latest.shape[0], LINES), :] = jnp.ones((latest.shape[0], CELLS), f32)
    centre_of[...] = cell[...].astype(f32) + offset[...]
    factor_of[...] = (-0.5 / math.log(2.0)) / (width[...] * width[...])
    particle = lax.broadcasted_iota(jnp.int32, (tiles, CELLS), 0) * CELLS + lanes_of(tiles)
    live_of[...] = jnp.where(particle < live[0:1, 0:1], rate[...], 0.0)
    turn = lanes_of(1) % CAP
    for t in range(tiles):
        slot = (latest[dest[t]] == t).astype(jnp.int32)
        first = dest[t] * LINES
        at = first + slot * EACH
        send[pl.ds(at, 1), :] = centre_of[t : t + 1, :]
        send[pl.ds(at + 1, 1), :] = factor_of[t : t + 1, :]
        send[pl.ds(at + 2, 1), :] = live_of[t : t + 1, :]
        send[pl.ds(at + 3, 4), :] = target[t]
        row_line = pl.ds(first + CAP * EACH, 1)
        send[row_line, :] = jnp.where(turn == slot, gas_row[t].astype(f32), send[row_line, :])


def turned(columns):
    lane = lanes_of(CELLS)
    total = jnp.zeros((CELLS, CELLS), f32)
    for i, column in enumerate(columns):
        total = jnp.where(lane == i, column, total)
    return total.T


def edge_columns(cells, first, lane):
    height = cells.shape[0] // VARS
    starts = [k * height + first + CELLS * b for k in (2, 3) for b in range((height - 2 * first) // CELLS)]
    return [cells[at : at + CELLS, lane : lane + 1] for at in starts]


def by_pair(first, second):
    even = lax.axis_index("axial") % 2 == 0
    return jnp.where(even, first, second), jnp.where(even, second, first)


def edges_kernel(state, flow, near, far, right, left):
    rows = flow.shape[0]
    ends = []
    for r in (0, rows - 1):
        lines = [state[k * rows + r : k * rows + r + 1, :] for k in range(VARS)]
        lines += [flow[r : r + 1, :], jnp.ones((3, CELLS), f32)]
        ends.append(jnp.concatenate(lines, 0))
    near[...], far[...] = by_pair(ends[1], ends[0])
    both = turned(edge_columns(state, 0, 0) + edge_columns(state, 0, CELLS - 1))
    left[...] = both[0:8, :]
    right[...] = both[8:16, :]


def chunk_rates(cells, flow, sides, r0, left_at, right_at):
    lane = lanes_of(CHUNK)
    starts = [k * (flow.shape[0] + 2 * TOP) + TOP + r0 for k in range(VARS)]
    dx = [0.5 * (cells[at + 1 : at + CHUNK + 1, :] - cells[at - 1 : at + CHUNK - 1, :]) for at in starts]
    dy = []
    block, within = r0 // CELLS, r0 % CELLS
    for k in (2, 3):
        cell = cells[starts[k] : starts[k] + CHUNK, :]
        if sides is None:
            before, after = 0.0, 0.0
        else:
            place = 4 * (k - 2) + block
            before = sides[within : within + CHUNK, left_at + place : left_at + place + 1]
            after = sides[within : within + CHUNK, right_at + place : right_at + place + 1]
        west = jnp.where(lane == 0, before, pltpu.roll(cell, 1, 1))
        east = jnp.where(lane == CELLS - 1, after, pltpu.roll(cell, CELLS - 1, 1))
        dy.append(0.5 * (east - west))
    speed = flow[r0 : r0 + CHUNK, :]
    spread = dx[1] + dy[0]
    return [
        -speed * dx[0] - spread,
        -speed * dx[1] - dx[3],
        -speed * dx[2] - dy[1],
        -speed * dx[3] - spread,
    ]


def at_row(k, r, rows):
    return k * (rows + 2 * TOP) + TOP + r


def fill_rows(cells, top, bottom):
    height = cells.shape[0] // VARS
    for k in range(VARS):
        cells[k * height + TOP - 1 : k * height + TOP, :] = top[k]
        cells[(k + 1) * height - TOP : (k + 1) * height - TOP + 1, :] = bottom[k]


def waves_kernel(state, flow, near, far, from_left, from_right, out, padded, sides):
    rows = flow.shape[0]
    below, above = by_pair(near[...], far[...])
    for k in range(VARS):
        padded[at_row(k, 0, rows) : at_row(k, rows, rows), :] = state[k * rows : (k + 1) * rows, :]
    fill_rows(padded, [above[k : k + 1, :] for k in range(VARS)], [below[k : k + 1, :] for k in range(VARS)])
    sides[...] = jnp.concatenate([from_left[...], from_right[...], jnp.zeros((CELLS - 16, CELLS), f32)], 0).T
    for r0 in range(0, rows, CHUNK):
        rates = chunk_rates(padded, flow, sides, r0, 0, 8)
        for k in range(VARS):
            here = state[k * rows + r0 : k * rows + r0 + CHUNK, :]
            out[at_row(k, r0, rows) : at_row(k, r0 + CHUNK, rows), :] = here + time_step * rates[k]
    fill_rows(out, [jnp.zeros((1, CELLS), f32)] * VARS, [jnp.zeros((1, CELLS), f32)] * VARS)


def sample(cells, first, row_of, samples):
    for t in range(samples.shape[0] // 8):
        lines = cells[pl.ds(row_of[0, t] + first, VARS, cells.shape[0] // VARS), :]
        samples[8 * t : 8 * t + 4, :] = lines
        samples[8 * t + 4 : 8 * t + 8, :] = lines


def high_and_low(values):
    high = values.astype(bf16).astype(f32)
    low_row = lax.broadcasted_iota(jnp.int32, values.shape, 0) % 8 >= 4
    return jnp.where(low_row, values - high, high)


def see_pair(samples, weights, sums, p):
    seen = high_and_low(samples[16 * p : 16 * p + 16, :]).astype(bf16)
    both = jnp.dot(jnp.concatenate([seen, seen], 1), weights[p], preferred_element_type=f32)
    for i in range(2):
        part = both[8 * i : 8 * i + 8, CELLS * i : CELLS * (i + 1)]
        sums[2 * p + i] = part + pltpu.roll(part, 4, 0)


def pair_sources(sums, turned_weights, goals, rates, scale, p):
    nothing = jnp.zeros((8, CELLS), f32)
    forces = [high_and_low(goals[t] - rates[t] * sums[t]) for t in (2 * p, 2 * p + 1)]
    forces = jnp.concatenate(
        [jnp.concatenate([forces[0], nothing], 1), jnp.concatenate([nothing, forces[1]], 1)], 0
    ).astype(bf16)
    both = jnp.dot(forces, turned_weights[p], preferred_element_type=f32)
    both = scale * (both[:, :CELLS] + both[:, CELLS:])
    return [both[8 * i : 8 * i + 4, :] + both[8 * i + 4 : 8 * i + 8, :] for i in range(2)]


def add_sources(sums, turned_weights, goals, rates, row_of, out, first, scale):
    for p in range(turned_weights.shape[0]):
        for i, part in enumerate(pair_sources(sums, turned_weights, goals, rates, scale, p)):
            lines = pl.ds(row_of[0, 2 * p + i] + first, VARS, out.shape[0] // VARS)
            out[lines, :] = out[lines, :] + part


def build_pair(got, weights, turned_weights, goals, rates, p):
    middle = lax.broadcasted_iota(jnp.int32, (CELLS, CELLS), 0).astype(f32) + 0.5
    for i in range(2):
        t = 2 * p + i
        at = p * LINES + i * EACH
        gap = middle - got[at : at + 1, :]
        weight = jnp.exp2(gap * gap * got[at + 1 : at + 2, :])
        whole = 1.0 / jnp.sum(weight, 0, keepdims=True)
        high = weight.astype(bf16)
        low = (weight - high.astype(f32)).astype(bf16)
        here = slice(CELLS * i, CELLS * (i + 1))
        weights[p, 0:CELLS, here] = high
        weights[p, CELLS : 2 * CELLS, here] = low
        turned_weights[p, here, 0:CELLS] = high.T
        turned_weights[p, here, CELLS : 2 * CELLS] = low.T
        scaled = got[at + 2 : at + 3, :] * whole
        target = got[at + 3 : at + 7, :]
        goals[t] = jnp.concatenate([target, target], 0) * scaled
        rates[t] = jnp.broadcast_to(scaled * whole, (8, CELLS))


def chunk_without_source(one, state, flow, r0):
    rows = flow.shape[0]
    change = chunk_rates(one, flow, None, r0, 0, 0)
    chunk = []
    for k in range(VARS):
        now = one[at_row(k, r0, rows) : at_row(k, r0 + CHUNK, rows), :]
        chunk.append(0.75 * state[k * rows + r0 : k * rows + r0 + CHUNK, :] + 0.25 * now + quarter * change[k])
    return chunk


def first_kernel(
    got, waves, state, flow, weights, turned_weights, goals, rates, row_list, one, samples, near, far,
    ends, sums, row_of, sem,
):
    pairs = got.shape[0] // LINES
    slots = CAP * pairs
    rows = flow.shape[0]
    lines = got[pl.ds(CAP * EACH, pairs, LINES), :]
    named = jnp.where(lax.broadcasted_iota(jnp.int32, (pairs, CELLS), 0) == lanes_of(pairs) // CAP, lines, 0.0)
    row_list[...] = jnp.broadcast_to(jnp.sum(named, 0, keepdims=True).astype(jnp.int32), (8, CELLS))
    copy = pltpu.make_async_copy(row_list, row_of, sem)
    copy.start()
    one[...] = waves[...]
    ahead = slots // 8
    for p in range(ahead):
        build_pair(got, weights, turned_weights, goals, rates, p)
    copy.wait()
    sample(state, 0, row_of, samples)
    for p in range(slots // 2):
        if p + ahead < slots // 2:
            build_pair(got, weights, turned_weights, goals, rates, p + ahead)
        see_pair(samples, weights, sums, p)
    add_sources(sums, turned_weights, goals, rates, row_of, one, TOP, time_step)
    sample(one, TOP, row_of, samples)
    start, end = (chunk_without_source(one, state, flow, r0) for r0 in (0, rows - CHUNK))
    ends[...] = jnp.concatenate([line[0:1, :] for line in start] + [line[CHUNK - 1 :, :] for line in end], 0)
    for p in range(pairs):
        at = [row_of[0, 2 * p + i] for i in range(2)]

        @pl.when((at[0] == 0) | (at[0] == rows - 1) | (at[1] == 0) | (at[1] == rows - 1))
        def _(p=p, at=at):
            see_pair(samples, weights, sums, p)
            for r, part in zip(at, pair_sources(sums, turned_weights, goals, rates, quarter, p)):
                ends[0:4, :] = ends[0:4, :] + jnp.where(r == 0, part, 0.0)
                ends[4:8, :] = ends[4:8, :] + jnp.where(r == rows - 1, part, 0.0)

    messages = []
    for r, start in ((0, 0), (rows - 1, 4)):
        lines = [one[at_row(k, r, rows) : at_row(k, r, rows) + 1, :] for k in range(VARS)]
        messages.append(jnp.concatenate(lines + [ends[start : start + 4, :]], 0))
    near[...], far[...] = by_pair(messages[1], messages[0])


def middle_kernel(
    row_of, one, samples, state, flow, weights, turned_weights, goals, rates, partial, right, left, sums
):
    rows = flow.shape[0]
    for p in range(weights.shape[0]):
        see_pair(samples, weights, sums, p)
    for r0 in range(0, rows, CHUNK):
        for k, chunk in enumerate(chunk_without_source(one, state, flow, r0)):
            partial[at_row(k, r0, rows) : at_row(k, r0 + CHUNK, rows), :] = chunk
    fill_rows(partial, [jnp.zeros((1, CELLS), f32)] * VARS, [jnp.zeros((1, CELLS), f32)] * VARS)
    add_sources(sums, turned_weights, goals, rates, row_of, partial, TOP, quarter)
    columns = []
    for lane in (0, CELLS - 1):
        columns += edge_columns(one, TOP, lane) + edge_columns(partial, TOP, lane)
    packs = turned(columns)
    left[...] = jnp.concatenate([packs[0:16, :], jnp.zeros((8, CELLS), f32)], 0)
    right[...] = jnp.concatenate([packs[16:32, :], jnp.zeros((8, CELLS), f32)], 0)


def across_rows(beside, flow_row, side):
    along = [beside[k : k + 1, :] for k in range(VARS)]
    factor = -side * eighth
    return [
        factor * (flow_row * along[0] + along[1]),
        factor * (flow_row * along[1] + along[3]),
        factor * (flow_row * along[2]),
        factor * (flow_row * along[3] + along[1]),
    ]


def columns_kernel(is_far, beside, flow, right_so_far, left_so_far, right, left):
    rows = flow.shape[0]
    last = rows // CELLS - 1
    lane = lanes_of(1)
    message = beside[...]
    nothing = jnp.zeros_like(message)
    below, above = by_pair(nothing, message) if is_far else by_pair(message, nothing)
    from_above = across_rows(above, flow[0:1, :], -1)
    from_below = across_rows(below, flow[rows - 1 : rows, :], 1)
    for out, before, at in ((left, left_so_far, 0), (right, right_so_far, CELLS - 1)):
        out[...] = before[...]
        for k in (2, 3):
            top, low = from_above[k], from_below[k]
            if at == 0:
                low = pltpu.roll(low, CELLS - 1, 1)
            else:
                top = pltpu.roll(top, 1, 1)
            r = 8 + 4 * (k - 2)
            out[r : r + 1, :] = out[r : r + 1, :] + jnp.where(lane == 0, top, 0.0)
            r = r + last
            out[r : r + 1, :] = out[r : r + 1, :] + jnp.where(lane == CELLS - 1, low, 0.0)
        for r, line in ((16, above[2:3, :]), (17, below[2:3, :]), (18, above[3:4, :]), (19, below[3:4, :])):
            out[r : r + 1, :] = out[r : r + 1, :] + line


def last_kernel(
    row_of, partial, state, flow, near, far, near_first, far_first, from_left, from_right,
    own_near, own_far, right, left, weights, turned_weights, goals, rates, out, two, sides, samples, sums,
):
    rows = flow.shape[0]
    lane = lanes_of(1)
    below, above = by_pair(near[...], far[...])
    below_first, above_first = by_pair(near_first[...], far_first[...])
    down, up = by_pair(own_near[...], own_far[...])
    own_left, own_right = left[0:8, :], right[0:8, :]
    halo_left = from_left[8:16, :] - eighth * jnp.concatenate([own_left[4:8, :], own_left[0:4, :]], 0)
    halo_right = from_right[8:16, :] + eighth * jnp.concatenate([own_right[4:8, :], own_right[0:4, :]], 0)
    sides[...] = jnp.concatenate(
        [from_left[0:8, :], from_right[0:8, :], halo_left, halo_right, jnp.zeros((CELLS - 32, CELLS), f32)], 0
    ).T

    def corner(west, east):
        return eighth * (
            jnp.where(lane == 0, pltpu.roll(west, 1, 1), 0.0)
            - jnp.where(lane == CELLS - 1, pltpu.roll(east, CELLS - 1, 1), 0.0)
        )

    halos = []
    for near, first, own, side, r in ((above, above_first, up, 1, 16), (below, below_first, down, -1, 17)):
        added = across_rows(own, first[4:5, :], side)
        v_term = corner(from_left[r : r + 1, :], from_right[r : r + 1, :])
        p_term = corner(from_left[r + 2 : r + 3, :], from_right[r + 2 : r + 3, :])
        turn = [v_term, 0.0, p_term, v_term]
        halos.append([first[5:6, :] * (near[4 + k : 5 + k, :] + added[k] + turn[k]) for k in range(VARS)])
    fill_rows(two, halos[0], halos[1])

    wide = lanes_of(CHUNK)
    for r0 in range(0, rows, CHUNK):
        block, within = r0 // CELLS, r0 % CELLS

        def beside(place):
            west = sides[within : within + CHUNK, place : place + 1]
            east = sides[within : within + CHUNK, 8 + place : 9 + place]
            return eighth * (jnp.where(wide == 0, west, 0.0) - jnp.where(wide == CELLS - 1, east, 0.0))

        v_term, p_term = beside(block), beside(4 + block)
        for k, term in enumerate((v_term, 0.0, p_term, v_term)):
            here = slice(at_row(k, r0, rows), at_row(k, r0 + CHUNK, rows))
            two[here, :] = partial[here, :] + term
    for near, r, side in ((above, 0, -1), (below, rows - 1, 1)):
        added = across_rows(near, flow[r : r + 1, :], side)
        for k in range(VARS):
            at = at_row(k, r, rows)
            two[at : at + 1, :] = two[at : at + 1, :] + added[k]

    sample(two, TOP, row_of, samples)
    for p in range(weights.shape[0]):
        see_pair(samples, weights, sums, p)
    for r0 in range(0, rows, CHUNK):
        change = chunk_rates(two, flow, sides, r0, 16, 24)
        for k in range(VARS):
            here = slice(k * rows + r0, k * rows + r0 + CHUNK)
            now = two[at_row(k, r0, rows) : at_row(k, r0 + CHUNK, rows), :]
            out[here, :] = state[here, :] / 3.0 + (2.0 / 3.0) * (now + time_step * change[k])
    add_sources(sums, turned_weights, goals, rates, row_of, out, 0, (2.0 / 3.0) * time_step)


def to_axial(near, far):
    count = lax.axis_size("axial")

    def pairs(start):
        return [move for i in range(start, count - 1, 2) for move in ((i, i + 1), (i + 1, i))]

    far = lax.ppermute(far, "axial", pairs(1))
    return lax.ppermute(near, "axial", pairs(0)), far


def to_azimuthal(right, left):
    count = lax.axis_size("azim")
    return (
        lax.ppermute(right, "azim", [(i, (i + 1) % count) for i in range(count)]),
        lax.ppermute(left, "azim", [((i + 1) % count, i) for i in range(count)]),
    )


def per_device(
    gas_state,
    mean_flow,
    part_target,
    part_offset,
    part_width,
    part_rate,
    cell_index,
    dest_owner,
    gas_row,
    live_count,
):
    sectors = lax.axis_size("azim")
    tiles = cell_index.shape[0]
    rows = gas_state.shape[1]
    slots = sectors * CAP
    pairs = slots // 2
    padded = (VARS * (rows + 2 * TOP), CELLS)
    state = gas_state.reshape(VARS * rows, CELLS)
    edge = shape((8, CELLS))

    send = pl.pallas_call(
        slots_kernel,
        out_shape=shape((sectors * LINES, CELLS)),
        in_specs=[smem()] * 2 + [vmem()] * 6,
        out_specs=vmem(),
        scratch_shapes=[pltpu.VMEM((tiles, CELLS), f32)] * 3 + [pltpu.SMEM((sectors,), jnp.int32)],
        name="slots",
    )(dest_owner[:, 0], gas_row, live_count.reshape(1, 1), part_target, part_offset, part_width, part_rate, cell_index)
    send = send.reshape(sectors, 1, LINES * CELLS)
    got = lax.all_to_all(send, "azim", split_axis=0, concat_axis=0, tiled=True).reshape(sectors * LINES, CELLS)

    near, far, right, left = pl.pallas_call(
        edges_kernel,
        out_shape=[edge] * 4,
        in_specs=[vmem()] * 2,
        out_specs=[vmem()] * 4,
        name="edges",
    )(state, mean_flow)
    near_first, far_first = to_axial(near, far)
    from_left, from_right = to_azimuthal(right, left)
    waves = pl.pallas_call(
        waves_kernel,
        out_shape=shape(padded),
        in_specs=[vmem()] * 6,
        out_specs=vmem(),
        scratch_shapes=[pltpu.VMEM(padded, f32), pltpu.VMEM((CELLS, CELLS), f32)],
        compiler_params=room(8),
        name="waves",
    )(state, mean_flow, near_first, far_first, from_left, from_right)

    weights, turned_weights, goals, rates, row_list, one, samples, own_near, own_far = pl.pallas_call(
        first_kernel,
        out_shape=[
            shape((pairs, 2 * CELLS, 2 * CELLS), bf16),
            shape((pairs, 2 * CELLS, 2 * CELLS), bf16),
            shape((slots, 8, CELLS)),
            shape((slots, 8, CELLS)),
            shape((8, CELLS), jnp.int32),
            shape(padded),
            shape((slots * 8, CELLS)),
            edge,
            edge,
        ],
        in_specs=[vmem()] * 4,
        out_specs=[vmem()] * 9,
        scratch_shapes=[
            pltpu.VMEM((8, CELLS), f32),
            pltpu.VMEM((slots, 8, CELLS), f32),
            pltpu.SMEM((8, CELLS), jnp.int32),
            pltpu.SemaphoreType.DMA,
        ],
        compiler_params=room(15),
        name="first",
    )(got, waves, state, mean_flow)
    near, far = to_axial(own_near, own_far)
    partial, own_right, own_left = pl.pallas_call(
        middle_kernel,
        out_shape=[shape(padded), shape((24, CELLS)), shape((24, CELLS))],
        in_specs=[smem()] + [vmem()] * 8,
        out_specs=[vmem()] * 3,
        scratch_shapes=[pltpu.VMEM((slots, 8, CELLS), f32)],
        compiler_params=room(15),
        name="middle",
    )(row_list, one, samples, state, mean_flow, weights, turned_weights, goals, rates)
    right, left = own_right, own_left
    for is_far, beside in ((True, far), (False, near)):
        right, left = pl.pallas_call(
            functools.partial(columns_kernel, is_far),
            out_shape=[shape((24, CELLS))] * 2,
            in_specs=[vmem()] * 4,
            out_specs=[vmem()] * 2,
            compiler_params=room(2),
            name="columns",
        )(beside, mean_flow, right, left)
    from_left, from_right = to_azimuthal(right, left)
    new_state = pl.pallas_call(
        last_kernel,
        out_shape=shape(state.shape),
        in_specs=[smem()] + [vmem()] * 17,
        out_specs=vmem(),
        scratch_shapes=[
            pltpu.VMEM(padded, f32),
            pltpu.VMEM((CELLS, CELLS), f32),
            pltpu.VMEM((slots * 8, CELLS), f32),
            pltpu.VMEM((slots, 8, CELLS), f32),
        ],
        compiler_params=room(15),
        name="last",
    )(
        row_list, partial, state, mean_flow, near, far, near_first, far_first, from_left, from_right,
        own_near, own_far, own_right, own_left, weights, turned_weights, goals, rates,
    )
    return new_state.reshape(gas_state.shape)


def solution(mesh):
    placed = (
        P(None, "axial", "azim"),
        P("axial", "azim"),
        P(("axial", "azim"), None, None),
        P(("axial", "azim"), None),
        P(("axial", "azim"), None),
        P(("axial", "azim"), None),
        P(("axial", "azim"), None),
        P(("axial", "azim"), None),
        P(("axial", "azim")),
        P(("axial", "azim")),
    )
    return jax.shard_map(
        per_device, mesh=mesh, in_specs=placed, out_specs=P(None, "axial", "azim"), check_vma=False
    )
```

```python
import functools
import math

import jax
import jax.numpy as jnp
from jax import lax
from jax.experimental import pallas as pl
from jax.experimental.pallas import tpu as pltpu
from jax.sharding import PartitionSpec as P

CAP = 2
CELLS = 128
VARS = 4
TOP = 8
CHUNK = 32
EACH = 7
LINES = CAP * EACH + 1
MIB = 1024 * 1024

time_step = 0.8
quarter = 0.25 * time_step
eighth = 0.125 * time_step

f32 = jnp.float32
bf16 = jnp.bfloat16


def vmem():
    return pl.BlockSpec(memory_space=pltpu.VMEM)


def smem():
    return pl.BlockSpec(memory_space=pltpu.SMEM)


def room(mib):
    return pltpu.CompilerParams(vmem_limit_bytes=mib * MIB)


def shape(dims, dtype=f32):
    return jax.ShapeDtypeStruct(dims, dtype)


def lanes_of(rows):
    return lax.broadcasted_iota(jnp.int32, (rows, CELLS), 1)


def slots_kernel(dest, gas_row, live, target, offset, width, rate, cell, send, centre_of, factor_of, live_of, latest):
    tiles = offset.shape[0]
    for t in range(tiles):
        latest[dest[t]] = t
    send[...] = jnp.zeros(send.shape, f32)
    send[pl.ds(CAP * EACH, latest.shape[0], LINES), :] = jnp.ones((latest.shape[0], CELLS), f32)
    centre_of[...] = cell[...].astype(f32) + offset[...]
    factor_of[...] = (-0.5 / math.log(2.0)) / (width[...] * width[...])
    particle = lax.broadcasted_iota(jnp.int32, (tiles, CELLS), 0) * CELLS + lanes_of(tiles)
    live_of[...] = jnp.where(particle < live[0:1, 0:1], rate[...], 0.0)
    turn = lanes_of(1) % CAP
    for t in range(tiles):
        slot = (latest[dest[t]] == t).astype(jnp.int32)
        first = dest[t] * LINES
        at = first + slot * EACH
        send[pl.ds(at, 1), :] = centre_of[t : t + 1, :]
        send[pl.ds(at + 1, 1), :] = factor_of[t : t + 1, :]
        send[pl.ds(at + 2, 1), :] = live_of[t : t + 1, :]
        send[pl.ds(at + 3, 4), :] = target[t]
        row_line = pl.ds(first + CAP * EACH, 1)
        send[row_line, :] = jnp.where(turn == slot, gas_row[t].astype(f32), send[row_line, :])


def turned(columns):
    lane = lanes_of(CELLS)
    total = jnp.zeros((CELLS, CELLS), f32)
    for i, column in enumerate(columns):
        total = jnp.where(lane == i, column, total)
    return total.T


def edge_columns(cells, first, lane):
    height = cells.shape[0] // VARS
    starts = [k * height + first + CELLS * b for k in (2, 3) for b in range((height - 2 * first) // CELLS)]
    return [cells[at : at + CELLS, lane : lane + 1] for at in starts]


def by_pair(first, second):
    even = lax.axis_index("axial") % 2 == 0
    return jnp.where(even, first, second), jnp.where(even, second, first)


def edges_kernel(state, flow, near, far, right, left):
    rows = flow.shape[0]
    ends = []
    for r in (0, rows - 1):
        lines = [state[k * rows + r : k * rows + r + 1, :] for k in range(VARS)]
        lines += [flow[r : r + 1, :], jnp.ones((3, CELLS), f32)]
        ends.append(jnp.concatenate(lines, 0))
    near[...], far[...] = by_pair(ends[1], ends[0])
    both = turned(edge_columns(state, 0, 0) + edge_columns(state, 0, CELLS - 1))
    left[...] = both[0:8, :]
    right[...] = both[8:16, :]


def chunk_rates(cells, flow, sides, r0, left_at, right_at):
    lane = lanes_of(CHUNK)
    starts = [k * (flow.shape[0] + 2 * TOP) + TOP + r0 for k in range(VARS)]
    dx = [0.5 * (cells[at + 1 : at + CHUNK + 1, :] - cells[at - 1 : at + CHUNK - 1, :]) for at in starts]
    dy = []
    block, within = r0 // CELLS, r0 % CELLS
    for k in (2, 3):
        cell = cells[starts[k] : starts[k] + CHUNK, :]
        if sides is None:
            before, after = 0.0, 0.0
        else:
            place = 4 * (k - 2) + block
            before = sides[within : within + CHUNK, left_at + place : left_at + place + 1]
            after = sides[within : within + CHUNK, right_at + place : right_at + place + 1]
        west = jnp.where(lane == 0, before, pltpu.roll(cell, 1, 1))
        east = jnp.where(lane == CELLS - 1, after, pltpu.roll(cell, CELLS - 1, 1))
        dy.append(0.5 * (east - west))
    speed = flow[r0 : r0 + CHUNK, :]
    spread = dx[1] + dy[0]
    return [
        -speed * dx[0] - spread,
        -speed * dx[1] - dx[3],
        -speed * dx[2] - dy[1],
        -speed * dx[3] - spread,
    ]


def at_row(k, r, rows):
    return k * (rows + 2 * TOP) + TOP + r


def fill_rows(cells, top, bottom):
    height = cells.shape[0] // VARS
    for k in range(VARS):
        cells[k * height + TOP - 1 : k * height + TOP, :] = top[k]
        cells[(k + 1) * height - TOP : (k + 1) * height - TOP + 1, :] = bottom[k]


def waves_kernel(state, flow, near, far, from_left, from_right, out, padded, sides):
    rows = flow.shape[0]
    below, above = by_pair(near[...], far[...])
    for k in range(VARS):
        padded[at_row(k, 0, rows) : at_row(k, rows, rows), :] = state[k * rows : (k + 1) * rows, :]
    fill_rows(padded, [above[k : k + 1, :] for k in range(VARS)], [below[k : k + 1, :] for k in range(VARS)])
    sides[...] = jnp.concatenate([from_left[...], from_right[...], jnp.zeros((CELLS - 16, CELLS), f32)], 0).T
    for r0 in range(0, rows, CHUNK):
        rates = chunk_rates(padded, flow, sides, r0, 0, 8)
        for k in range(VARS):
            here = state[k * rows + r0 : k * rows + r0 + CHUNK, :]
            out[at_row(k, r0, rows) : at_row(k, r0 + CHUNK, rows), :] = here + time_step * rates[k]
    fill_rows(out, [jnp.zeros((1, CELLS), f32)] * VARS, [jnp.zeros((1, CELLS), f32)] * VARS)


def sample(cells, first, row_of, samples):
    for t in range(samples.shape[0] // 8):
        lines = cells[pl.ds(row_of[0, t] + first, VARS, cells.shape[0] // VARS), :]
        samples[8 * t : 8 * t + 4, :] = lines
        samples[8 * t + 4 : 8 * t + 8, :] = lines


def high_and_low(values):
    high = values.astype(bf16).astype(f32)
    low_row = lax.broadcasted_iota(jnp.int32, values.shape, 0) % 8 >= 4
    return jnp.where(low_row, values - high, high)


def see_pair(samples, weights, sums, p):
    seen = high_and_low(samples[16 * p : 16 * p + 16, :]).astype(bf16)
    both = jnp.dot(jnp.concatenate([seen, seen], 1), weights[p], preferred_element_type=f32)
    for i in range(2):
        part = both[8 * i : 8 * i + 8, CELLS * i : CELLS * (i + 1)]
        sums[2 * p + i] = part + pltpu.roll(part, 4, 0)


def pair_sources(sums, turned_weights, goals, rates, scale, p):
    nothing = jnp.zeros((8, CELLS), f32)
    forces = [high_and_low(goals[t] - rates[t] * sums[t]) for t in (2 * p, 2 * p + 1)]
    forces = jnp.concatenate(
        [jnp.concatenate([forces[0], nothing], 1), jnp.concatenate([nothing, forces[1]], 1)], 0
    ).astype(bf16)
    both = jnp.dot(forces, turned_weights[p], preferred_element_type=f32)
    both = scale * (both[:, :CELLS] + both[:, CELLS:])
    return [both[8 * i : 8 * i + 4, :] + both[8 * i + 4 : 8 * i + 8, :] for i in range(2)]


def add_sources(sums, turned_weights, goals, rates, row_of, out, first, scale):
    for p in range(turned_weights.shape[0]):
        for i, part in enumerate(pair_sources(sums, turned_weights, goals, rates, scale, p)):
            lines = pl.ds(row_of[0, 2 * p + i] + first, VARS, out.shape[0] // VARS)
            out[lines, :] = out[lines, :] + part


def build_pair(got, weights, turned_weights, goals, rates, p):
    middle = lax.broadcasted_iota(jnp.int32, (CELLS, CELLS), 0).astype(f32) + 0.5
    for i in range(2):
        t = 2 * p + i
        at = p * LINES + i * EACH
        gap = middle - got[at : at + 1, :]
        weight = jnp.exp2(gap * gap * got[at + 1 : at + 2, :])
        whole = 1.0 / jnp.sum(weight, 0, keepdims=True)
        high = weight.astype(bf16)
        low = (weight - high.astype(f32)).astype(bf16)
        here = slice(CELLS * i, CELLS * (i + 1))
        weights[p, 0:CELLS, here] = high
        weights[p, CELLS : 2 * CELLS, here] = low
        turned_weights[p, here, 0:CELLS] = high.T
        turned_weights[p, here, CELLS : 2 * CELLS] = low.T
        scaled = got[at + 2 : at + 3, :] * whole
        target = got[at + 3 : at + 7, :]
        goals[t] = jnp.concatenate([target, target], 0) * scaled
        rates[t] = jnp.broadcast_to(scaled * whole, (8, CELLS))


def chunk_without_source(one, state, flow, r0):
    rows = flow.shape[0]
    change = chunk_rates(one, flow, None, r0, 0, 0)
    chunk = []
    for k in range(VARS):
        now = one[at_row(k, r0, rows) : at_row(k, r0 + CHUNK, rows), :]
        chunk.append(0.75 * state[k * rows + r0 : k * rows + r0 + CHUNK, :] + 0.25 * now + quarter * change[k])
    return chunk


def first_kernel(
    got, waves, state, flow, weights, turned_weights, goals, rates, row_list, one, samples, near, far,
    ends, sums, row_of, sem,
):
    pairs = got.shape[0] // LINES
    slots = CAP * pairs
    rows = flow.shape[0]
    lines = got[pl.ds(CAP * EACH, pairs, LINES), :]
    named = jnp.where(lax.broadcasted_iota(jnp.int32, (pairs, CELLS), 0) == lanes_of(pairs) // CAP, lines, 0.0)
    row_list[...] = jnp.broadcast_to(jnp.sum(named, 0, keepdims=True).astype(jnp.int32), (8, CELLS))
    copy = pltpu.make_async_copy(row_list, row_of, sem)
    copy.start()
    one[...] = waves[...]
    ahead = slots // 8
    for p in range(ahead):
        build_pair(got, weights, turned_weights, goals, rates, p)
    copy.wait()
    sample(state, 0, row_of, samples)
    for p in range(slots // 2):
        if p + ahead < slots // 2:
            build_pair(got, weights, turned_weights, goals, rates, p + ahead)
        see_pair(samples, weights, sums, p)
    add_sources(sums, turned_weights, goals, rates, row_of, one, TOP, time_step)
    sample(one, TOP, row_of, samples)
    start, end = (chunk_without_source(one, state, flow, r0) for r0 in (0, rows - CHUNK))
    ends[...] = jnp.concatenate([line[0:1, :] for line in start] + [line[CHUNK - 1 :, :] for line in end], 0)
    places = [row_of[0, t] for t in range(slots)]
    outer = [((r == 0) | (r == rows - 1)).astype(jnp.int32) for r in places]

    @pl.when(functools.reduce(jnp.add, outer) > 0)
    def _():
        for p in range(pairs):

            @pl.when(outer[2 * p] + outer[2 * p + 1] > 0)
            def _(p=p):
                see_pair(samples, weights, sums, p)
                for i, part in enumerate(pair_sources(sums, turned_weights, goals, rates, quarter, p)):
                    r = row_of[0, 2 * p + i]
                    ends[0:4, :] = ends[0:4, :] + jnp.where(r == 0, part, 0.0)
                    ends[4:8, :] = ends[4:8, :] + jnp.where(r == rows - 1, part, 0.0)

    messages = []
    for r, start in ((0, 0), (rows - 1, 4)):
        lines = [one[at_row(k, r, rows) : at_row(k, r, rows) + 1, :] for k in range(VARS)]
        messages.append(jnp.concatenate(lines + [ends[start : start + 4, :]], 0))
    near[...], far[...] = by_pair(messages[1], messages[0])


def middle_kernel(
    row_of, one, samples, state, flow, weights, turned_weights, goals, rates, partial, right, left, sums
):
    rows = flow.shape[0]
    for p in range(weights.shape[0]):
        see_pair(samples, weights, sums, p)
    for r0 in range(0, rows, CHUNK):
        for k, chunk in enumerate(chunk_without_source(one, state, flow, r0)):
            partial[at_row(k, r0, rows) : at_row(k, r0 + CHUNK, rows), :] = chunk
    fill_rows(partial, [jnp.zeros((1, CELLS), f32)] * VARS, [jnp.zeros((1, CELLS), f32)] * VARS)
    add_sources(sums, turned_weights, goals, rates, row_of, partial, TOP, quarter)
    columns = []
    for lane in (0, CELLS - 1):
        columns += edge_columns(one, TOP, lane) + edge_columns(partial, TOP, lane)
    packs = turned(columns)
    left[...] = jnp.concatenate([packs[0:16, :], jnp.zeros((8, CELLS), f32)], 0)
    right[...] = jnp.concatenate([packs[16:32, :], jnp.zeros((8, CELLS), f32)], 0)


def across_rows(beside, flow_row, side):
    along = [beside[k : k + 1, :] for k in range(VARS)]
    factor = -side * eighth
    return [
        factor * (flow_row * along[0] + along[1]),
        factor * (flow_row * along[1] + along[3]),
        factor * (flow_row * along[2]),
        factor * (flow_row * along[3] + along[1]),
    ]


def columns_kernel(is_far, beside, flow, right_so_far, left_so_far, right, left):
    rows = flow.shape[0]
    last = rows // CELLS - 1
    lane = lanes_of(1)
    message = beside[...]
    nothing = jnp.zeros_like(message)
    below, above = by_pair(nothing, message) if is_far else by_pair(message, nothing)
    from_above = across_rows(above, flow[0:1, :], -1)
    from_below = across_rows(below, flow[rows - 1 : rows, :], 1)
    for out, before, at in ((left, left_so_far, 0), (right, right_so_far, CELLS - 1)):
        out[...] = before[...]
        for k in (2, 3):
            top, low = from_above[k], from_below[k]
            if at == 0:
                low = pltpu.roll(low, CELLS - 1, 1)
            else:
                top = pltpu.roll(top, 1, 1)
            r = 8 + 4 * (k - 2)
            out[r : r + 1, :] = out[r : r + 1, :] + jnp.where(lane == 0, top, 0.0)
            r = r + last
            out[r : r + 1, :] = out[r : r + 1, :] + jnp.where(lane == CELLS - 1, low, 0.0)
        for r, line in ((16, above[2:3, :]), (17, below[2:3, :]), (18, above[3:4, :]), (19, below[3:4, :])):
            out[r : r + 1, :] = out[r : r + 1, :] + line


def last_kernel(
    row_of, partial, state, flow, near, far, near_first, far_first, from_left, from_right,
    own_near, own_far, right, left, weights, turned_weights, goals, rates, out, two, sides, samples, sums,
):
    rows = flow.shape[0]
    lane = lanes_of(1)
    below, above = by_pair(near[...], far[...])
    below_first, above_first = by_pair(near_first[...], far_first[...])
    down, up = by_pair(own_near[...], own_far[...])
    own_left, own_right = left[0:8, :], right[0:8, :]
    halo_left = from_left[8:16, :] - eighth * jnp.concatenate([own_left[4:8, :], own_left[0:4, :]], 0)
    halo_right = from_right[8:16, :] + eighth * jnp.concatenate([own_right[4:8, :], own_right[0:4, :]], 0)
    sides[...] = jnp.concatenate(
        [from_left[0:8, :], from_right[0:8, :], halo_left, halo_right, jnp.zeros((CELLS - 32, CELLS), f32)], 0
    ).T

    def corner(west, east):
        return eighth * (
            jnp.where(lane == 0, pltpu.roll(west, 1, 1), 0.0)
            - jnp.where(lane == CELLS - 1, pltpu.roll(east, CELLS - 1, 1), 0.0)
        )

    halos = []
    for near, first, own, side, r in ((above, above_first, up, 1, 16), (below, below_first, down, -1, 17)):
        added = across_rows(own, first[4:5, :], side)
        v_term = corner(from_left[r : r + 1, :], from_right[r : r + 1, :])
        p_term = corner(from_left[r + 2 : r + 3, :], from_right[r + 2 : r + 3, :])
        turn = [v_term, 0.0, p_term, v_term]
        halos.append([first[5:6, :] * (near[4 + k : 5 + k, :] + added[k] + turn[k]) for k in range(VARS)])
    fill_rows(two, halos[0], halos[1])

    wide = lanes_of(CHUNK)
    for r0 in range(0, rows, CHUNK):
        block, within = r0 // CELLS, r0 % CELLS

        def beside(place):
            west = sides[within : within + CHUNK, place : place + 1]
            east = sides[within : within + CHUNK, 8 + place : 9 + place]
            return eighth * (jnp.where(wide == 0, west, 0.0) - jnp.where(wide == CELLS - 1, east, 0.0))

        v_term, p_term = beside(block), beside(4 + block)
        for k, term in enumerate((v_term, 0.0, p_term, v_term)):
            here = slice(at_row(k, r0, rows), at_row(k, r0 + CHUNK, rows))
            two[here, :] = partial[here, :] + term
    for near, r, side in ((above, 0, -1), (below, rows - 1, 1)):
        added = across_rows(near, flow[r : r + 1, :], side)
        for k in range(VARS):
            at = at_row(k, r, rows)
            two[at : at + 1, :] = two[at : at + 1, :] + added[k]

    sample(two, TOP, row_of, samples)
    for p in range(weights.shape[0]):
        see_pair(samples, weights, sums, p)
    for r0 in range(0, rows, CHUNK):
        change = chunk_rates(two, flow, sides, r0, 16, 24)
        for k in range(VARS):
            here = slice(k * rows + r0, k * rows + r0 + CHUNK)
            now = two[at_row(k, r0, rows) : at_row(k, r0 + CHUNK, rows), :]
            out[here, :] = state[here, :] / 3.0 + (2.0 / 3.0) * (now + time_step * change[k])
    add_sources(sums, turned_weights, goals, rates, row_of, out, 0, (2.0 / 3.0) * time_step)


def to_axial(near, far):
    count = lax.axis_size("axial")

    def pairs(start):
        return [move for i in range(start, count - 1, 2) for move in ((i, i + 1), (i + 1, i))]

    far = lax.ppermute(far, "axial", pairs(1))
    return lax.ppermute(near, "axial", pairs(0)), far


def to_azimuthal(right, left):
    count = lax.axis_size("azim")
    return (
        lax.ppermute(right, "azim", [(i, (i + 1) % count) for i in range(count)]),
        lax.ppermute(left, "azim", [((i + 1) % count, i) for i in range(count)]),
    )


def per_device(
    gas_state,
    mean_flow,
    part_target,
    part_offset,
    part_width,
    part_rate,
    cell_index,
    dest_owner,
    gas_row,
    live_count,
):
    sectors = lax.axis_size("azim")
    tiles = cell_index.shape[0]
    rows = gas_state.shape[1]
    slots = sectors * CAP
    pairs = slots // 2
    padded = (VARS * (rows + 2 * TOP), CELLS)
    state = gas_state.reshape(VARS * rows, CELLS)
    edge = shape((8, CELLS))

    send = pl.pallas_call(
        slots_kernel,
        out_shape=shape((sectors * LINES, CELLS)),
        in_specs=[smem()] * 2 + [vmem()] * 6,
        out_specs=vmem(),
        scratch_shapes=[pltpu.VMEM((tiles, CELLS), f32)] * 3 + [pltpu.SMEM((sectors,), jnp.int32)],
        name="slots",
    )(dest_owner[:, 0], gas_row, live_count.reshape(1, 1), part_target, part_offset, part_width, part_rate, cell_index)
    send = send.reshape(sectors, 1, LINES * CELLS)
    got = lax.all_to_all(send, "azim", split_axis=0, concat_axis=0, tiled=True).reshape(sectors * LINES, CELLS)

    near, far, right, left = pl.pallas_call(
        edges_kernel,
        out_shape=[edge] * 4,
        in_specs=[vmem()] * 2,
        out_specs=[vmem()] * 4,
        name="edges",
    )(state, mean_flow)
    near_first, far_first = to_axial(near, far)
    from_left, from_right = to_azimuthal(right, left)
    waves = pl.pallas_call(
        waves_kernel,
        out_shape=shape(padded),
        in_specs=[vmem()] * 6,
        out_specs=vmem(),
        scratch_shapes=[pltpu.VMEM(padded, f32), pltpu.VMEM((CELLS, CELLS), f32)],
        compiler_params=room(8),
        name="waves",
    )(state, mean_flow, near_first, far_first, from_left, from_right)

    weights, turned_weights, goals, rates, row_list, one, samples, own_near, own_far = pl.pallas_call(
        first_kernel,
        out_shape=[
            shape((pairs, 2 * CELLS, 2 * CELLS), bf16),
            shape((pairs, 2 * CELLS, 2 * CELLS), bf16),
            shape((slots, 8, CELLS)),
            shape((slots, 8, CELLS)),
            shape((8, CELLS), jnp.int32),
            shape(padded),
            shape((slots * 8, CELLS)),
            edge,
            edge,
        ],
        in_specs=[vmem()] * 4,
        out_specs=[vmem()] * 9,
        scratch_shapes=[
            pltpu.VMEM((8, CELLS), f32),
            pltpu.VMEM((slots, 8, CELLS), f32),
            pltpu.SMEM((8, CELLS), jnp.int32),
            pltpu.SemaphoreType.DMA,
        ],
        compiler_params=room(15),
        name="first",
    )(got, waves, state, mean_flow)
    near, far = to_axial(own_near, own_far)
    partial, own_right, own_left = pl.pallas_call(
        middle_kernel,
        out_shape=[shape(padded), shape((24, CELLS)), shape((24, CELLS))],
        in_specs=[smem()] + [vmem()] * 8,
        out_specs=[vmem()] * 3,
        scratch_shapes=[pltpu.VMEM((slots, 8, CELLS), f32)],
        compiler_params=room(15),
        name="middle",
    )(row_list, one, samples, state, mean_flow, weights, turned_weights, goals, rates)
    right, left = own_right, own_left
    for is_far, beside in ((True, far), (False, near)):
        right, left = pl.pallas_call(
            functools.partial(columns_kernel, is_far),
            out_shape=[shape((24, CELLS))] * 2,
            in_specs=[vmem()] * 4,
            out_specs=[vmem()] * 2,
            compiler_params=room(2),
            name="columns",
        )(beside, mean_flow, right, left)
    from_left, from_right = to_azimuthal(right, left)
    new_state = pl.pallas_call(
        last_kernel,
        out_shape=shape(state.shape),
        in_specs=[smem()] + [vmem()] * 17,
        out_specs=vmem(),
        scratch_shapes=[
            pltpu.VMEM(padded, f32),
            pltpu.VMEM((CELLS, CELLS), f32),
            pltpu.VMEM((slots * 8, CELLS), f32),
            pltpu.VMEM((slots, 8, CELLS), f32),
        ],
        compiler_params=room(15),
        name="last",
    )(
        row_list, partial, state, mean_flow, near, far, near_first, far_first, from_left, from_right,
        own_near, own_far, own_right, own_left, weights, turned_weights, goals, rates,
    )
    return new_state.reshape(gas_state.shape)


def solution(mesh):
    placed = (
        P(None, "axial", "azim"),
        P("axial", "azim"),
        P(("axial", "azim"), None, None),
        P(("axial", "azim"), None),
        P(("axial", "azim"), None),
        P(("axial", "azim"), None),
        P(("axial", "azim"), None),
        P(("axial", "azim"), None),
        P(("axial", "azim")),
        P(("axial", "azim")),
    )
    return jax.shard_map(
        per_device, mesh=mesh, in_specs=placed, out_specs=P(None, "axial", "azim"), check_vma=False
    )
```
